128 devices in a mesh: owner: 64 (over z, y, x), sub: 2 (over core).
Axes of the slice: x: 4, y: 4, z: 4, core: 2. Of those that a mesh axis runs over, the one named last changes fastest.
Arguments:
- file_fields: bfloat16 [131072, 2560], P(('owner', 'sub')), may hold values from -6 to 6
- span_map: int32 [128, 128], P(('owner', 'sub')), may hold values from 0 to 127, each once within a row
- point_dest: int32 [2097152, 1], P(('owner', 'sub')), may hold values from 0 to 127; in each aligned block of 16384 rows (0 to 16383, 16384 to 32767, ...) at most 256 rows name the same one
- point_local: int32 [2097152], P(('owner', 'sub')), may hold values from 0 to 1023, as said below
- point_coords: float32 [3, 2097152], P(None, ('owner', 'sub')), may hold values from -1 to 1
Outputs:
- point_values: float32 [5, 2097152], P(None, ('owner', 'sub'))
- owned: bfloat16 [131072, 2560], P(('owner', 'sub'))
The draws below stay inside these ranges and needn't reach their ends.
Inputs may be any that keep to these rules, and one draw needn't show every extreme that they name: `point_dest`: among the 16384 points of one device at most 256 name one owner, a bound that some blocks reach. `span_map`: each row is a permutation of the owners. Among the 16384 points of one device at most 192 have the same point_local // 8, and some value of it is taken by exactly 192 of them.
All inputs are finite; a program needn't handle non-finite values.
Results may differ from the reference program's by a relative error of at most 0.001.
Values may be sent and summed in bfloat16 or wider, within the bound.
No kernel may reach another device: no remote copies, remote signals or barrier semaphores. Data moves between devices by JAX's collectives and lax.ppermute only.
A program may use at most 128 MiB of HBM per device.

```python
import math
import jax
import jax.numpy as jnp
import numpy as np
from jax import lax

FIELDS = 5
NODES = 8
SPAN = 8
P_DEV = 16384
E_DEV = 1024
ELEMENTS = 131072
POINTS = 2097152
CAP = 256
DEVICES = 128


def draw_point_local(key, part):
    key = jax.random.fold_in(key, 7)
    rounds = P_DEV // DEVICES
    keys = jax.random.split(key, DEVICES)

    def one_block(block_key):
        first_key, second_key, third_key = jax.random.split(block_key, 3)
        shuffle = jax.random.permutation(first_key, DEVICES).astype(jnp.int32)
        order = jax.random.permutation(second_key, P_DEV).astype(jnp.int32)
        column = order % DEVICES
        turn = order // DEVICES
        index = jnp.where(turn < rounds // 2, column, column - column % 2)
        holder = shuffle[index]
        within = jax.random.randint(third_key, (P_DEV,), 0, SPAN).astype(jnp.int32)
        return (holder * SPAN + within).astype(jnp.int32)
    return jax.vmap(one_block)(keys).reshape(POINTS)


def block_scale(key, dims, cuts, low, top_value):
    def one(dim, parts):
        draws = jax.random.uniform(jax.random.fold_in(jax.random.fold_in(key, 6), dim), (parts,), jnp.float32, low / len(cuts), top_value / len(cuts))
        return jnp.repeat(jnp.exp(draws), dims[dim] // parts).reshape((-1,) + (1,) * (len(dims) - dim - 1))

    factor_of = one(*cuts[0])
    for cut in cuts[1:]:
        factor_of = factor_of * one(*cut)
    return factor_of


def routed_block(own_key, own, number, rows, amount, top, most, lean):
    ranking = jax.random.permutation(own_key, amount)
    heavy_load, ordinary = portions_of(amount, rows * top, most, lean, True), portions_of(amount, rows * top, most, lean, False)
    places = jnp.arange(amount)

    def named(tallies, rotation):
        used = int((tallies > 0).sum())
        fixed = max(1, used // 4)
        moved = fixed + (places - fixed + rotation * (used - fixed)) % max(1, amount - fixed)
        return jnp.zeros((amount,), jnp.int32).at[ranking[jnp.where(places < fixed, places, moved)]].set(jnp.asarray(tallies, jnp.int32))

    tallies = jnp.where(number % 4 == 0, named(heavy_load, number // 4), named(ordinary, number - number // 4 - 1))
    mixed = jax.random.permutation(jax.random.fold_in(own, 3), amount)
    source_of, sink = mixed[0:amount // 2 * 2:2], mixed[1:amount // 2 * 2:2]
    margin = jnp.minimum(tallies[source_of] - 1, most - tallies[sink]) // 2
    margin = jnp.where((source_of == ranking[0]) | (sink == ranking[0]) | (tallies[sink] == 0), 0, jnp.maximum(margin, 0))
    moved = jax.random.randint(jax.random.fold_in(own, 4), (amount // 2,), 0, 1 << 20) % (margin + 1)
    tallies = tallies.at[source_of].add(-moved).at[sink].add(moved)
    items = jnp.searchsorted(jnp.cumsum(tallies), jnp.arange(rows * top), side="right").astype(jnp.int32)
    table = items.reshape(top, rows).T
    table = table[jax.random.permutation(jax.random.fold_in(own, 1), rows)]
    rotation = jax.random.randint(jax.random.fold_in(own, 2), (rows, 1), 0, top)
    return jnp.take_along_axis(table, (jnp.arange(top)[None, :] + rotation) % top, axis=1)


def portions_of(amount, total, bound, slope, full):
    weights = [(1 << 20) // math.isqrt(grade ** slope) + 1 for grade in range(1, amount + 1)]
    largest = bound if full else min(bound, max(-(-total // amount), total * weights[0] // sum(weights)))
    least = 1 if total - largest >= amount - 1 else 0
    holding, rest = [largest] + [least] * (amount - 1), total - largest - least * (amount - 1)
    while rest > 0:
        candidates = [i for i in range(1, amount) if holding[i] < largest] or [i for i in range(1, amount) if holding[i] < bound]
        whole, left = sum([weights[i] for i in candidates]), rest
        for i in candidates:
            extra = min(bound - holding[i], max(1, left * weights[i] // whole), rest)
            holding[i] = holding[i] + extra
            rest = rest - extra
    return np.array(holding)


def normal_values(key, shape, scale, bound, cuts=(), kind=jnp.bfloat16):
    factor_of = block_scale(key, shape, cuts, -0.22, 0.18) if cuts else 1.0
    drawn = jax.random.normal(key, shape, jnp.float32) * scale * factor_of
    return jnp.minimum(jnp.maximum(drawn, -bound), bound).astype(kind)


def setup_inputs(seed: int = 0) -> dict:
    arg_keys = jax.random.split(jax.random.key(seed), 6)
    file_fields = normal_values(arg_keys[0], (ELEMENTS, FIELDS * NODES ** 3), 1.0, 6.0, ((0, 128),))
    span_map = jax.vmap(lambda own: jax.random.permutation(own, DEVICES))(jax.random.split(arg_keys[1], DEVICES)).reshape((DEVICES, DEVICES)).astype(jnp.int32)
    point_dest_keys = jax.random.split(jax.random.fold_in(arg_keys[2], 1), POINTS // P_DEV)
    point_dest_turns = jax.random.permutation(jax.random.fold_in(arg_keys[2], 3), POINTS // P_DEV)
    point_dest = jax.vmap(lambda own, number: routed_block(jax.random.fold_in(arg_keys[2], 2), own, number, P_DEV, DEVICES, 1, CAP, 2))(point_dest_keys, point_dest_turns).reshape((POINTS, 1))
    point_local = draw_point_local(jax.random.fold_in(arg_keys[5], 71), 0)
    point_coords = jnp.clip(jax.random.uniform(arg_keys[4], (3, POINTS), jnp.float32, -1.0, 1.0) * block_scale(arg_keys[4], (3, POINTS), ((1, 128),), -0.4, 0.0), -1.0, 1.0)
    return dict(file_fields=file_fields, span_map=span_map, point_dest=point_dest, point_local=point_local, point_coords=point_coords)


def gll_nodes(count):
    order = count - 1
    points = np.cos(np.pi * np.arange(count) / order)
    for sweep in range(100):
        oldest = np.ones(count)
        recent = points * 1.0
        for degree in range(2, order + 1):
            newest = ((2 * degree - 1) * points * recent - (degree - 1) * oldest) / degree
            oldest = recent
            recent = newest
        points = points - (points * recent - oldest) / (count * recent)
    return points[::-1]


def lagrange(coords, nodes):
    count = nodes.shape[0]
    result = []
    for i in range(count):
        term = jnp.ones_like(coords)
        for j in range(count):
            if j != i:
                term = term * ((coords - float(nodes[j])) * float(1.0 / (nodes[i] - nodes[j])))
        result.append(term)
    return jnp.stack(result, 0)


def evaluate(element_rows, basis):
    count = basis.shape[1]
    block = basis.shape[2]
    first, second, third = basis[0], basis[1], basis[2]
    tensor = (first[:, None, None, :] * second[None, :, None, :] * third[None, None, :, :]).reshape(count ** 3, block)
    values = element_rows.reshape(block, -1, count ** 3).astype(jnp.float32)
    return jnp.sum(values * tensor.T[:, None, :], axis=2).T


def reference(file_fields, span_map, point_dest, point_local, point_coords):
    nodes = gll_nodes(NODES)
    columns = jnp.arange(DEVICES, dtype=jnp.int32)
    inverse = jnp.zeros((DEVICES, DEVICES), jnp.int32).at[columns[:, None], span_map].set(
        jnp.broadcast_to(columns[None, :], (DEVICES, DEVICES)))
    width = file_fields.shape[1]
    arranged = file_fields.reshape(DEVICES, DEVICES, SPAN, width)
    owned = arranged[columns[None, :], inverse.T].reshape(ELEMENTS, width)
    destination = point_dest[:, 0]
    holder = point_local // SPAN
    within = point_local % SPAN
    file_row = (holder * E_DEV + inverse[holder, destination] * SPAN + within).astype(jnp.int32)
    basis = jnp.moveaxis(lagrange(point_coords.astype(jnp.float32), nodes), 0, 1)
    block = min(4096, POINTS)
    number = POINTS // block
    row_blocks = file_row.reshape(number, block)
    basis_blocks = basis.reshape(3, NODES, number, block).transpose(2, 0, 1, 3)
    result = lax.map(lambda item: evaluate(file_fields[item[0]], item[1]), (row_blocks, basis_blocks))
    return result.transpose(1, 0, 2).reshape(FIELDS, POINTS), owned
```

```python
import jax
import jax.numpy as jnp
import numpy as np
from jax import lax
from jax.experimental import pallas as pl
from jax.experimental.pallas import tpu as pltpu
from jax.sharding import PartitionSpec as P

NODES = 8
FIELDS = 5
SPAN = 8
DEVICES = 128
POINTS = 16384
CAP = 192
HALF = 64
WIDTH = FIELDS * NODES**3
SLOTS = DEVICES * CAP
GROUP = 64
GROUPS = 16
TILE = 256
AXES = ("owner", "sub")
F32 = jnp.float32
BF16 = jnp.bfloat16
I32 = jnp.int32


def gll_nodes(count):
    order = count - 1
    points = np.cos(np.pi * np.arange(count) / order)
    for sweep in range(100):
        oldest = np.ones(count)
        recent = points * 1.0
        for degree in range(2, order + 1):
            newest = ((2 * degree - 1) * points * recent - (degree - 1) * oldest) / degree
            oldest = recent
            recent = newest
        points = points - (points * recent - oldest) / (count * recent)
    return points[::-1]


def iota(shape, dim):
    return lax.broadcasted_iota(I32, shape, dim)


def lane_dot(a, b):
    return lax.dot_general(a, b, (((1,), (1,)), ((), ())), preferred_element_type=F32)


def dot(a, b):
    return jnp.dot(a, b, preferred_element_type=F32)


def parts(x):
    high = x.astype(BF16).astype(F32)
    return high, x - high


def earlier(rows, cols):
    return jnp.where(iota((rows, cols), 0) < iota((rows, cols), 1), 1.0, 0.0).astype(BF16)


def ranks(mask, before, base):
    ones = jnp.where(mask, 1.0, 0.0)
    narrow = ones.astype(BF16)
    counts = []
    for j in range(mask.shape[1] // 256):
        part = slice(256 * j, 256 * j + 256)
        inside = dot(narrow[:, part], before)
        counts.append(inside + base)
        base = base + inside[:, 255:256] + ones[:, 256 * j + 255 : 256 * j + 256]
    count = jnp.concatenate(counts, axis=1)
    return jnp.sum(jnp.where(mask, count, 0.0), axis=0, keepdims=True), base


def spread(mask, value):
    return jnp.where(mask, value, 0.0).astype(BF16)


A_LANES = 1024


def bucket_kernel(dest_ref, local_ref, coords_ref, out_ref, pos_ref, acc_ref):
    acc_ref[...] = jnp.zeros_like(acc_ref)
    before = earlier(256, 256)

    def step(n, base):
        lanes = pl.ds(pl.multiple_of(n * A_LANES, A_LANES), A_LANES)
        local = local_ref[:, lanes]
        mask = iota((DEVICES, A_LANES), 0) == (local >> 3)
        pos, base = ranks(mask, before, base)
        pos = pos.astype(I32)
        pos_ref[:, lanes] = pos
        place = jnp.where(iota((256, A_LANES), 0) == pos, 1.0, 0.0).astype(BF16)
        wide = jnp.concatenate([place, place], axis=1)
        rows = []
        for k in range(3):
            high, low = parts(coords_ref[k : k + 1, lanes])
            rows.append(jnp.concatenate([spread(mask, high), spread(mask, low)], axis=1))
        high = (dest_ref[:, lanes] * 8 + 8).astype(F32)
        low = (local & 7).astype(F32)
        rows.append(jnp.concatenate([spread(mask, high), spread(mask, low)], axis=1))
        acc_ref[...] += lane_dot(jnp.concatenate(rows, axis=0), wide)
        return base

    lax.fori_loop(0, POINTS // A_LANES, step, jnp.zeros((DEVICES, 1), F32))
    for k in range(4):
        out_ref[:, k, :] = acc_ref[k * 128 : k * 128 + 128, 0:128]
        out_ref[:, 4 + k, :] = acc_ref[k * 128 : k * 128 + 128, 128:256]


def bucket(dest, local, coords):
    return pl.pallas_call(
        bucket_kernel,
        out_shape=(
            jax.ShapeDtypeStruct((DEVICES, 8, 128), F32),
            jax.ShapeDtypeStruct((1, POINTS), I32),
        ),
        in_specs=[pl.BlockSpec(memory_space=pltpu.VMEM)] * 3,
        out_specs=(pl.BlockSpec(memory_space=pltpu.VMEM),) * 2,
        scratch_shapes=[pltpu.VMEM((512, 256), F32)],
        compiler_params=pltpu.CompilerParams(vmem_limit_bytes=48 * 1024 * 1024),
        name="bucket",
    )(dest, local, coords)


SOURCES = 8
C_LANES = SOURCES * CAP
STEPS = DEVICES // SOURCES


def basis_rows(x, nodes, scale):
    row = iota((8, x.shape[1]), 0)
    out = None
    for n in range(8):
        term = jnp.where(row == n, scale, x - float(nodes[n]))
        out = term if out is None else out * term
    return out


def evaluate_kernel(
    recv_ref, span_ref, file_ref, out_ref, flat_ref, sorted_ref, slot_ref, val_ref, acc_ref, first_ref
):
    nodes = gll_nodes(NODES)
    before = earlier(256, 256)
    inverse = jnp.sum(
        jnp.where(iota((128, 128), 0) == span_ref[...], iota((128, 128), 1), 0).astype(F32),
        axis=1,
        keepdims=True,
    )
    lane = iota((8, 128), 1)

    def count(n, base):
        source = n * SOURCES
        blocks = [recv_ref[source + s] for s in range(SOURCES)]
        pairs = [
            jnp.where(lane < HALF, blocks[2 * s], pltpu.roll(blocks[2 * s + 1], HALF, 1))
            for s in range(SOURCES // 2)
        ]
        full = jnp.concatenate(blocks, axis=1)[0:4]
        rest = jnp.concatenate(pairs, axis=1)[4:8]
        data = jnp.concatenate([full, rest], axis=1)
        number = data[3:4].astype(I32)
        mask = iota((128, C_LANES), 0) == (number >> 3) - 1
        span = jnp.sum(jnp.where(mask, inverse, 0.0), axis=0, keepdims=True).astype(I32)
        group = jnp.where(number > 0, span >> 3, GROUPS)
        element = (span & 7) * 8 + (number & 7)
        rank, base = ranks(iota((GROUPS, C_LANES), 0) == group, before, base)
        lanes = pl.ds(pl.multiple_of(n * C_LANES, C_LANES), C_LANES)
        flat_ref[0:3, lanes] = data[0:3]
        flat_ref[3:4, lanes] = element.astype(F32)
        flat_ref[4:5, lanes] = group.astype(F32)
        flat_ref[5:6, lanes] = rank
        return base

    total = lax.fori_loop(0, STEPS, count, jnp.zeros((GROUPS, 1), F32))
    tiles = ((total.astype(I32) + (TILE - 1)) >> 8).astype(F32)
    lower = jnp.where(iota((GROUPS, GROUPS), 1) < iota((GROUPS, GROUPS), 0), 1.0, 0.0)
    start = dot(lower.astype(BF16), jnp.broadcast_to(tiles, (GROUPS, 128)).astype(BF16))[:, 0:1]
    for g in range(GROUPS):
        first_ref[g] = jnp.sum(start[g : g + 1]).astype(I32)
    first_ref[GROUPS] = jnp.sum(tiles).astype(I32)

    sorted_ref[...] = jnp.zeros_like(sorted_ref)
    slot_ref[...] = jnp.zeros_like(slot_ref)

    def sort(n, carry):
        lanes = pl.ds(pl.multiple_of(n * C_LANES, C_LANES), C_LANES)
        group = flat_ref[4:5, lanes].astype(I32)
        here = iota((GROUPS, C_LANES), 0) == group
        base = jnp.sum(jnp.where(here, start, 0.0), axis=0, keepdims=True)
        slot = base.astype(I32) * TILE + flat_ref[5:6, lanes].astype(I32)
        high = jnp.where(group < GROUPS, slot >> 8, -1)
        mask = iota((128, C_LANES), 0) == high
        place = jnp.where(iota((TILE, C_LANES), 0) == (slot & 255), 1.0, 0.0).astype(BF16)
        at = iota((1, C_LANES), 1)
        late = at - SOURCES * 128
        second = late >= 0
        source = n * SOURCES + jnp.where(second, late >> 6, at >> 7)
        column = jnp.where(second, 128 + (late & 63), at & 127).astype(F32)
        rows = []
        for k in range(3):
            top, low = parts(flat_ref[k : k + 1, lanes])
            rows.append(jnp.concatenate([spread(mask, top), spread(mask, low)], axis=1))
        top = ((source + 1) * 64).astype(F32)
        rows.append(
            jnp.concatenate([spread(mask, top), spread(mask, flat_ref[3:4, lanes])], axis=1)
        )
        wide = jnp.concatenate([place, place], axis=1)
        sorted_ref[...] += lane_dot(jnp.concatenate(rows, axis=0), wide)
        slot_ref[...] += lane_dot(spread(mask, column), place)
        return carry

    lax.fori_loop(0, STEPS, sort, 0)

    val_ref[...] = jnp.zeros_like(val_ref)
    scale = []
    for i in range(8):
        value = 1.0
        for n in range(8):
            if n != i:
                value = value / (nodes[i] - nodes[n])
        scale.append(float(value))
    row8 = iota((8, TILE), 0)
    scales = jnp.zeros((8, TILE), F32)
    for i in range(8):
        scales = jnp.where(row8 == i, scale[i], scales)

    def on_group(g, carry):
        rows = pl.ds(pl.multiple_of(g * GROUP, GROUP), GROUP)
        table = jnp.concatenate(
            [file_ref[rows, f * 512 : f * 512 + 512] for f in range(FIELDS)], axis=0
        )
        table = jnp.concatenate([table, table], axis=1)

        def on_tile(t, inner):
            b0 = basis_rows(sorted_ref[pl.ds(t, 1), :], nodes, scales)
            b1 = basis_rows(sorted_ref[pl.ds(128 + t, 1), :], nodes, scales)
            b2 = basis_rows(sorted_ref[pl.ds(256 + t, 1), :], nodes, scales)
            element = sorted_ref[pl.ds(384 + t, 1), :].astype(I32) & 63
            planes = jnp.concatenate([b1[j : j + 1] * b2 for j in range(8)], axis=0)
            tops, lows = [], []
            for i in range(8):
                tensor = b0[i : i + 1] * planes
                top = tensor.astype(BF16)
                tops.append(top)
                lows.append((tensor - top.astype(F32)).astype(BF16))
            result = dot(table, jnp.concatenate(tops + lows, axis=0))
            mask = iota((GROUP, TILE), 0) == element
            for f in range(FIELDS):
                part = result[f * GROUP : f * GROUP + GROUP]
                val_ref[pl.ds(f * 128 + t, 1), :] = jnp.sum(
                    jnp.where(mask, part, 0.0), axis=0, keepdims=True
                )
            return inner

        return lax.fori_loop(first_ref[g], first_ref[g + 1], on_tile, carry)

    lax.fori_loop(0, GROUPS, on_group, 0)

    acc_ref[...] = jnp.zeros_like(acc_ref)
    many = 4

    def back(n, carry):
        def row(ref, at):
            lines = [ref[pl.ds(at + n * many + q, 1), :] for q in range(many)]
            return jnp.concatenate(lines, axis=1)

        source = (row(sorted_ref, 384).astype(I32) >> 6) - 1
        column = row(slot_ref, 0).astype(I32)
        mask = iota((128, many * TILE), 0) == source
        place = jnp.where(iota((256, many * TILE), 0) == column, 1.0, 0.0).astype(BF16)
        wide = jnp.concatenate([place, place], axis=1)
        rows = []
        for f in range(FIELDS):
            top, low = parts(row(val_ref, f * 128))
            rows.append(jnp.concatenate([spread(mask, top), spread(mask, low)], axis=1))
        acc_ref[...] += lane_dot(jnp.concatenate(rows, axis=0), wide)
        return carry

    lax.fori_loop(0, (first_ref[GROUPS] + many - 1) // many, back, 0)
    late = []
    for f in range(FIELDS):
        out_ref[:, f, :] = acc_ref[f * 128 : f * 128 + 128, 0:128]
        late.append(acc_ref[f * 128 : f * 128 + 128, 128:256])
    late.append(jnp.zeros_like(late[0]))
    low = iota((128, 128), 1) < HALF
    for f in range(3):
        out_ref[:, FIELDS + f, :] = jnp.where(low, late[2 * f], pltpu.roll(late[2 * f + 1], HALF, 1))


def evaluate(recv, span, file_fields):
    return pl.pallas_call(
        evaluate_kernel,
        out_shape=jax.ShapeDtypeStruct((DEVICES, 8, 128), F32),
        in_specs=[pl.BlockSpec(memory_space=pltpu.VMEM)] * 3,
        out_specs=pl.BlockSpec(memory_space=pltpu.VMEM),
        scratch_shapes=[
            pltpu.VMEM((8, SLOTS), F32),
            pltpu.VMEM((512, TILE), F32),
            pltpu.VMEM((128, TILE), F32),
            pltpu.VMEM((FIELDS * 128, TILE), F32),
            pltpu.VMEM((FIELDS * 128, 256), F32),
            pltpu.SMEM((GROUPS + 1,), I32),
        ],
        compiler_params=pltpu.CompilerParams(vmem_limit_bytes=56 * 1024 * 1024),
        cost_estimate=pl.CostEstimate(
            flops=60_000_000_000, bytes_accessed=6_000_000, transcendentals=0
        ),
        name="evaluate",
    )(recv, span, file_fields)


E_LANES = 256


def collect_kernel(back_ref, local_ref, pos_ref, out_ref, table_ref):
    for f in range(FIELDS):
        first = back_ref[:, f, :]
        second = back_ref[:, FIELDS + f // 2, :]
        if f % 2:
            second = pltpu.roll(second, HALF, 1)
        high, low = parts(jnp.concatenate([first, second], axis=1))
        table_ref[f * 128 : f * 128 + 128, 0:256] = high.astype(BF16)
        table_ref[f * 128 : f * 128 + 128, 256:512] = low.astype(BF16)

    def step(n, carry):
        lanes = pl.ds(pl.multiple_of(n * E_LANES, E_LANES), E_LANES)
        mask = iota((128, E_LANES), 0) == (local_ref[:, lanes] >> 3)
        place = jnp.where(iota((256, E_LANES), 0) == pos_ref[:, lanes], 1.0, 0.0).astype(BF16)
        got = dot(table_ref[...], jnp.concatenate([place, place], axis=0))
        for f in range(FIELDS):
            out_ref[f : f + 1, lanes] = jnp.sum(
                jnp.where(mask, got[f * 128 : f * 128 + 128], 0.0), axis=0, keepdims=True
            )
        return carry

    lax.fori_loop(0, POINTS // E_LANES, step, 0)


def collect(back, local, pos):
    return pl.pallas_call(
        collect_kernel,
        out_shape=jax.ShapeDtypeStruct((FIELDS, POINTS), F32),
        in_specs=[pl.BlockSpec(memory_space=pltpu.VMEM)] * 3,
        out_specs=pl.BlockSpec(memory_space=pltpu.VMEM),
        scratch_shapes=[pltpu.VMEM((FIELDS * 128, 512), BF16)],
        compiler_params=pltpu.CompilerParams(vmem_limit_bytes=48 * 1024 * 1024),
        name="collect",
    )(back, local, pos)


def exchange(x):
    return lax.all_to_all(x, AXES, split_axis=0, concat_axis=0, tiled=True)


def shards(file_fields, span_map, point_dest, point_local, point_coords):
    columns = jnp.arange(DEVICES, dtype=I32)
    inverse = jnp.zeros((DEVICES,), I32).at[span_map[0]].set(columns)
    pieces = file_fields.reshape(DEVICES, SPAN, WIDTH)[inverse]
    local = point_local.reshape(1, POINTS)
    sent, pos = bucket(point_dest.reshape(1, POINTS), local, point_coords)
    recv = exchange(sent)
    pieces, recv = lax.optimization_barrier((pieces, recv))
    owned = exchange(pieces).reshape(DEVICES * SPAN, WIDTH)
    values = evaluate(recv, span_map, file_fields)
    back = exchange(values)
    return collect(back, local, pos), owned


def solution(mesh):
    return jax.shard_map(
        shards,
        mesh=mesh,
        in_specs=(
            P(AXES, None),
            P(AXES, None),
            P(AXES, None),
            P(AXES),
            P(None, AXES),
        ),
        out_specs=(P(None, AXES), P(AXES, None)),
        check_vma=False,
    )
```

```python
import jax
import jax.numpy as jnp
import numpy as np
from jax import lax
from jax.experimental import pallas as pl
from jax.experimental.pallas import tpu as pltpu
from jax.sharding import PartitionSpec as P

NODES = 8
FIELDS = 5
SPAN = 8
DEVICES = 128
POINTS = 16384
CAP = 192
HALF = 64
WIDTH = FIELDS * NODES**3
SLOTS = DEVICES * CAP
GROUP = 64
GROUPS = 16
TILE = 256
ROWS = SLOTS // 256
MOST = SLOTS // TILE + GROUPS
AXES = ("owner", "sub")
F32 = jnp.float32
BF16 = jnp.bfloat16
I32 = jnp.int32


def gll_nodes(count):
    order = count - 1
    points = np.cos(np.pi * np.arange(count) / order)
    for sweep in range(100):
        oldest = np.ones(count)
        recent = points * 1.0
        for degree in range(2, order + 1):
            newest = ((2 * degree - 1) * points * recent - (degree - 1) * oldest) / degree
            oldest = recent
            recent = newest
        points = points - (points * recent - oldest) / (count * recent)
    return points[::-1]


def iota(shape, dim):
    return lax.broadcasted_iota(I32, shape, dim)


def lane_dot(a, b):
    return lax.dot_general(a, b, (((1,), (1,)), ((), ())), preferred_element_type=F32)


def dot(a, b):
    return jnp.dot(a, b, preferred_element_type=F32)


def parts(x):
    high = x.astype(BF16).astype(F32)
    return high, x - high


def earlier(rows, cols):
    return jnp.where(iota((rows, cols), 0) < iota((rows, cols), 1), 1.0, 0.0).astype(BF16)


def packed(value):
    return jnp.broadcast_to(value.astype(F32), (16, value.shape[1])).astype(BF16)


def onehot(first, rows, value):
    value = packed(value)
    base = iota(value.shape, 0)
    one, zero = jnp.asarray(1.0, BF16), jnp.asarray(0.0, BF16)
    out = []
    for r in range(rows // 16):
        out.append(jnp.where((base + (first + 16 * r)).astype(F32).astype(BF16) == value, one, zero))
    return jnp.concatenate(out, axis=0)


def spread(ones, value):
    value = packed(value)
    return jnp.concatenate(
        [ones[16 * r : 16 * r + 16] * value for r in range(ones.shape[0] // 16)], axis=0
    )


def both(ones, high, low):
    return jnp.concatenate([spread(ones, high), spread(ones, low)], axis=1)


def ranks(mask, before, base):
    ones = jnp.where(mask, 1.0, 0.0)
    narrow = ones.astype(BF16)
    counts = []
    for j in range(mask.shape[1] // 256):
        part = slice(256 * j, 256 * j + 256)
        inside = dot(narrow[:, part], before)
        counts.append(inside + base)
        base = base + inside[:, 255:256] + ones[:, 256 * j + 255 : 256 * j + 256]
    count = jnp.concatenate(counts, axis=1)
    return jnp.sum(jnp.where(mask, count, 0.0), axis=0, keepdims=True), base


def flat_slot(block, place):
    odd = (block & 1) == 1
    late = place >= 128
    return block * CAP + jnp.where(odd, jnp.where(late, place - 128, place + 64), place)


A_LANES = 2048


def bucket_kernel(
    dest_hbm, local_hbm, coords_hbm, out_ref, slot_ref, dest_ref, local_ref, coords_ref, acc_ref, flat_ref, sems
):
    copies = [
        pltpu.make_async_copy(src, dst, sems.at[n])
        for n, (src, dst) in enumerate(
            [(local_hbm, local_ref), (dest_hbm, dest_ref), (coords_hbm, coords_ref)]
        )
    ]
    for copy in copies:
        copy.start()
    acc_ref[...] = jnp.zeros_like(acc_ref)
    before = earlier(256, 256)
    steps = POINTS // A_LANES

    def at(n):
        return pl.ds(pl.multiple_of(n * A_LANES, A_LANES), A_LANES)

    def place(n, base):
        holder = local_ref[:, at(n)] >> 3
        rank, base = ranks(iota((DEVICES, A_LANES), 0) == holder, before, base)
        slot_ref[:, at(n)] = flat_slot(holder, rank.astype(I32))
        return base

    def scatter(n):
        slot = slot_ref[:, at(n)]
        where_row = onehot(0, ROWS, slot >> 8)
        where_col = onehot(0, 256, slot & 255)
        rows = [both(where_row, *parts(coords_ref[k : k + 1, at(n)])) for k in range(3)]
        rows.append(both(where_row, dest_ref[:, at(n)] * 8 + 8, local_ref[:, at(n)] & 7))
        wide = jnp.concatenate([where_col, where_col], axis=1)
        return lane_dot(jnp.concatenate(rows, axis=0), wide)

    copies[0].wait()
    base = place(0, jnp.zeros((DEVICES, 1), F32))
    copies[1].wait()
    copies[2].wait()

    def step(n, base):
        got = scatter(n)
        base = place(n + 1, base)
        acc_ref[...] += got
        return base

    lax.fori_loop(0, steps - 1, step, base)
    acc_ref[...] += scatter(steps - 1)
    for k in range(4):
        block = acc_ref[k * ROWS : k * ROWS + ROWS, :]
        flat_ref[pl.ds(0, ROWS, 2), :] = block[:, 0:128]
        flat_ref[pl.ds(1, ROWS, 2), :] = block[:, 128:256]
        out_ref[:, k, :] = flat_ref[pl.ds(0, 64, 3), :]
        out_ref[:, 8 + k, :] = flat_ref[pl.ds(2, 64, 3), :]
        middle = flat_ref[pl.ds(1, 64, 3), :]
        out_ref[:, 4 + k, :] = middle
        out_ref[:, 12 + k, :] = pltpu.roll(middle, HALF, 1)


def bucket(dest, local, coords):
    return pl.pallas_call(
        bucket_kernel,
        out_shape=(
            jax.ShapeDtypeStruct((DEVICES // 2, 16, 128), F32),
            jax.ShapeDtypeStruct((1, POINTS), I32),
        ),
        in_specs=[pl.BlockSpec(memory_space=pl.ANY)] * 3,
        out_specs=(pl.BlockSpec(memory_space=pltpu.VMEM),) * 2,
        scratch_shapes=[
            pltpu.VMEM((1, POINTS), I32),
            pltpu.VMEM((1, POINTS), I32),
            pltpu.VMEM((3, POINTS), F32),
            pltpu.VMEM((4 * ROWS, 256), F32),
            pltpu.VMEM((2 * ROWS, 128), F32),
            pltpu.SemaphoreType.DMA((3,)),
        ],
        compiler_params=pltpu.CompilerParams(vmem_limit_bytes=56 * 1024 * 1024),
        name="bucket",
    )(dest, local, coords)


SOURCES = 16
C_LANES = SOURCES * CAP
STEPS = DEVICES // SOURCES
USUAL = 96
PAIR = 2
MANY = 8


def basis_rows(x, nodes, scale):
    row = iota((8, x.shape[1]), 0)
    out = None
    for n in range(8):
        term = jnp.where(row == n, scale, x - float(nodes[n]))
        out = term if out is None else out * term
    return out


def evaluate_kernel(
    recv_ref, span_ref, file_hbm, out_ref, file_ref, data_ref, sorted_ref, val_ref, acc_ref, flat_ref, first_ref, group_ref, sem
):
    load = pltpu.make_async_copy(file_hbm, file_ref, sem)
    load.start()
    nodes = gll_nodes(NODES)
    before = earlier(256, 256)
    permutation = jnp.where(iota((128, 128), 0) == span_ref[...], 1.0, 0.0).astype(BF16)
    inverse = lane_dot(iota((16, 128), 1).astype(F32).astype(BF16), permutation).astype(BF16)
    lane = iota((8, 128), 1)

    def count(n, base):
        source = n * SOURCES
        blocks = [recv_ref[source + s] for s in range(SOURCES)]
        pairs = [
            jnp.where(lane < HALF, blocks[2 * s], pltpu.roll(blocks[2 * s + 1], HALF, 1))
            for s in range(SOURCES // 2)
        ]
        full = jnp.concatenate(blocks, axis=1)[0:4]
        rest = jnp.concatenate(pairs, axis=1)[4:8]
        data = jnp.concatenate([full, rest], axis=1)
        number = data[3:4].astype(I32)
        span = dot(inverse, onehot(0, 128, (number >> 3) - 1))[0:1].astype(I32)
        group = jnp.where(number > 0, span >> 3, GROUPS)
        element = (span & 7) * 8 + (number & 7)
        rank, base = ranks(iota((GROUPS, C_LANES), 0) == group, before, base)
        lanes = pl.ds(pl.multiple_of(n * C_LANES, C_LANES), C_LANES)
        data_ref[0:3, lanes] = data[0:3]
        data_ref[3:4, lanes] = element.astype(F32)
        data_ref[4:5, lanes] = group.astype(F32)
        data_ref[5:6, lanes] = rank
        return base

    total = lax.fori_loop(0, STEPS, count, jnp.zeros((GROUPS, 1), F32))
    tiles = ((total.astype(I32) + (TILE - 1)) >> 8).astype(F32)
    lower = jnp.where(iota((GROUPS, GROUPS), 1) < iota((GROUPS, GROUPS), 0), 1.0, 0.0)
    start = dot(lower.astype(BF16), jnp.broadcast_to(tiles, (GROUPS, 128)).astype(BF16))[:, 0:1]
    for g in range(GROUPS):
        first_ref[g] = jnp.sum(start[g : g + 1]).astype(I32)
    first_ref[GROUPS] = jnp.sum(tiles).astype(I32)
    used = first_ref[GROUPS]

    def name_group(g, carry):
        def name_tile(t, inner):
            group_ref[t] = g
            return inner

        return lax.fori_loop(first_ref[g], first_ref[g + 1], name_tile, carry)

    lax.fori_loop(0, GROUPS, name_group, 0)
    for n in range(PAIR - 1):
        group_ref[used + n] = 0

    sorted_ref[...] = jnp.zeros_like(sorted_ref)

    def sort(n, first, rows):
        lanes = pl.ds(pl.multiple_of(n * C_LANES, C_LANES), C_LANES)
        group = data_ref[4:5, lanes].astype(I32)
        here = iota((GROUPS, C_LANES), 0) == group
        base = jnp.sum(jnp.where(here, start, 0.0), axis=0, keepdims=True)
        slot = base.astype(I32) * TILE + data_ref[5:6, lanes].astype(I32)
        where_row = onehot(first, rows, jnp.where(group < GROUPS, slot >> 8, -1))
        where_col = onehot(0, TILE, slot & 255)
        at = iota((1, C_LANES), 1)
        late = at - SOURCES * 128
        second = late >= 0
        source = n * SOURCES + jnp.where(second, late >> 6, at >> 7)
        back = flat_slot(source, jnp.where(second, 128 + (late & 63), at & 127))
        lhs = [both(where_row, *parts(data_ref[k : k + 1, lanes])) for k in range(3)]
        lhs.append(both(where_row, ((back >> 8) + 1) * 64, data_ref[3:4, lanes]))
        wide = jnp.concatenate([where_col, where_col], axis=1)
        got = lane_dot(jnp.concatenate(lhs, axis=0), wide)
        last = lane_dot(spread(where_row, back & 255), where_col)
        for k in range(4):
            sorted_ref[k, first : first + rows, :] += got[k * rows : k * rows + rows]
        sorted_ref[4, first : first + rows, :] += last

    def usual(n, carry):
        sort(n, 0, USUAL)
        return carry

    lax.fori_loop(0, STEPS, usual, 0)

    @pl.when(used > USUAL)
    def _():
        def more(n, carry):
            sort(n, USUAL, MOST - USUAL)
            return carry

        lax.fori_loop(0, STEPS, more, 0)

    val_ref[...] = jnp.zeros_like(val_ref)
    load.wait()
    row8 = iota((8, TILE), 0)
    scales = jnp.zeros((8, TILE), F32)
    for i in range(8):
        value = 1.0
        for n in range(8):
            if n != i:
                value = value / (nodes[i] - nodes[n])
        scales = jnp.where(row8 == i, float(value), scales)

    def one_tile(t):
        rows = pl.ds(pl.multiple_of(group_ref[t] * GROUP, GROUP), GROUP)
        table = jnp.concatenate(
            [file_ref[rows, f * 512 : f * 512 + 512] for f in range(FIELDS)], axis=0
        )
        table = jnp.concatenate([table, table], axis=1)
        b0, b1, b2 = [basis_rows(sorted_ref[k, pl.ds(t, 1), :], nodes, scales) for k in range(3)]
        element = sorted_ref[3, pl.ds(t, 1), :].astype(I32) & 63
        planes = jnp.concatenate([b1[j : j + 1] * b2 for j in range(8)], axis=0)
        tops, lows = [], []
        for i in range(8):
            tensor = b0[i : i + 1] * planes
            top = tensor.astype(BF16)
            tops.append(top)
            lows.append((tensor - top.astype(F32)).astype(BF16))
        result = dot(table, jnp.concatenate(tops + lows, axis=0))
        mask = iota((GROUP, TILE), 0) == element
        return [
            jnp.sum(
                jnp.where(mask, result[f * GROUP : f * GROUP + GROUP], 0.0), axis=0, keepdims=True
            )
            for f in range(FIELDS)
        ]

    def on_tiles(n, carry):
        values = [one_tile(n * PAIR + q) for q in range(PAIR)]
        for q in range(PAIR):
            for f in range(FIELDS):
                val_ref[f, pl.ds(n * PAIR + q, 1), :] = values[q][f]
        return carry

    lax.fori_loop(0, (used + PAIR - 1) // PAIR, on_tiles, 0)

    acc_ref[...] = jnp.zeros_like(acc_ref)

    def back(n, carry):
        def row(ref, k):
            lines = [ref[k, pl.ds(n * MANY + q, 1), :] for q in range(MANY)]
            return jnp.concatenate(lines, axis=1)

        where_row = onehot(0, ROWS, (row(sorted_ref, 3).astype(I32) >> 6) - 1)
        where_col = onehot(0, 256, row(sorted_ref, 4))
        wide = jnp.concatenate([where_col, where_col], axis=1)
        lhs = [both(where_row, *parts(row(val_ref, f))) for f in range(FIELDS)]
        acc_ref[...] += lane_dot(jnp.concatenate(lhs, axis=0), wide)
        return carry

    lax.fori_loop(0, (used + MANY - 1) // MANY, back, 0)
    middle = []
    for f in range(FIELDS):
        block = acc_ref[f * ROWS : f * ROWS + ROWS, :]
        flat_ref[pl.ds(0, ROWS, 2), :] = block[:, 0:128]
        flat_ref[pl.ds(1, ROWS, 2), :] = block[:, 128:256]
        out_ref[:, f, :] = flat_ref[pl.ds(0, 64, 3), :]
        out_ref[:, 8 + f, :] = flat_ref[pl.ds(2, 64, 3), :]
        middle.append(flat_ref[pl.ds(1, 64, 3), :])
    middle.append(jnp.zeros_like(middle[0]))
    low = iota((64, 128), 1) < HALF
    for k in range(3):
        left, right = middle[2 * k], middle[2 * k + 1]
        out_ref[:, 5 + k, :] = jnp.where(low, left, pltpu.roll(right, HALF, 1))
        out_ref[:, 13 + k, :] = jnp.where(low, pltpu.roll(left, HALF, 1), right)


def evaluate(recv, span, file_fields):
    return pl.pallas_call(
        evaluate_kernel,
        out_shape=jax.ShapeDtypeStruct((DEVICES // 2, 16, 128), F32),
        in_specs=[
            pl.BlockSpec(memory_space=pltpu.VMEM),
            pl.BlockSpec(memory_space=pltpu.VMEM),
            pl.BlockSpec(memory_space=pl.ANY),
        ],
        out_specs=pl.BlockSpec(memory_space=pltpu.VMEM),
        scratch_shapes=[
            pltpu.VMEM((DEVICES * SPAN, WIDTH), BF16),
            pltpu.VMEM((8, SLOTS), F32),
            pltpu.VMEM((5, MOST, TILE), F32),
            pltpu.VMEM((FIELDS, MOST, TILE), F32),
            pltpu.VMEM((FIELDS * ROWS, 256), F32),
            pltpu.VMEM((2 * ROWS, 128), F32),
            pltpu.SMEM((GROUPS + 1,), I32),
            pltpu.SMEM((MOST + PAIR,), I32),
            pltpu.SemaphoreType.DMA(()),
        ],
        compiler_params=pltpu.CompilerParams(vmem_limit_bytes=56 * 1024 * 1024),
        cost_estimate=pl.CostEstimate(
            flops=60_000_000_000, bytes_accessed=6_000_000, transcendentals=0
        ),
        name="evaluate",
    )(recv, span, file_fields)


E_LANES = 2048
PIECES = 4


def collect_kernel(
    back_ref, slot_ref, moved_hbm, out_ref, owned_hbm, table_ref, flat_ref, held_ref, sems
):
    rows = DEVICES * SPAN // PIECES
    pieces = [pl.ds(n * rows, rows) for n in range(PIECES)]
    loads = [
        pltpu.make_async_copy(moved_hbm.at[p], held_ref.at[p], sems.at[n])
        for n, p in enumerate(pieces)
    ]
    stores = [
        pltpu.make_async_copy(held_ref.at[p], owned_hbm.at[p], sems.at[PIECES + n])
        for n, p in enumerate(pieces)
    ]
    for copy in loads:
        copy.start()
    low = iota((64, 128), 1) < HALF
    for f in range(FIELDS):
        flat_ref[pl.ds(0, 64, 3), :] = back_ref[:, f, :]
        flat_ref[pl.ds(2, 64, 3), :] = back_ref[:, 8 + f, :]
        left, right = back_ref[:, 5 + f // 2, :], back_ref[:, 13 + f // 2, :]
        if f % 2:
            left = pltpu.roll(left, HALF, 1)
        else:
            right = pltpu.roll(right, HALF, 1)
        flat_ref[pl.ds(1, 64, 3), :] = jnp.where(low, left, right)
        for half in range(2):
            high, rest = parts(flat_ref[pl.ds(half, ROWS, 2), :])
            here = slice(f * ROWS, f * ROWS + ROWS)
            table_ref[here, 128 * half : 128 * half + 128] = high.astype(BF16)
            table_ref[here, 256 + 128 * half : 384 + 128 * half] = rest.astype(BF16)

    def step(n, carry):
        lanes = pl.ds(pl.multiple_of(n * E_LANES, E_LANES), E_LANES)
        slot = slot_ref[:, lanes]
        mask = iota((ROWS, E_LANES), 0) == (slot >> 8)
        where_col = onehot(0, 256, slot & 255)
        got = dot(table_ref[...], jnp.concatenate([where_col, where_col], axis=0))
        for f in range(FIELDS):
            out_ref[f : f + 1, lanes] = jnp.sum(
                jnp.where(mask, got[f * ROWS : f * ROWS + ROWS], 0.0), axis=0, keepdims=True
            )
        return carry

    steps = POINTS // E_LANES
    lax.fori_loop(0, steps // 2, step, 0)
    for load, store in zip(loads, stores):
        load.wait()
        store.start()
    lax.fori_loop(steps // 2, steps, step, 0)
    for store in stores:
        store.wait()


def collect(back, slot, moved):
    return pl.pallas_call(
        collect_kernel,
        out_shape=(
            jax.ShapeDtypeStruct((FIELDS, POINTS), F32),
            jax.ShapeDtypeStruct(moved.shape, moved.dtype),
        ),
        in_specs=[
            pl.BlockSpec(memory_space=pltpu.VMEM),
            pl.BlockSpec(memory_space=pltpu.VMEM),
            pl.BlockSpec(memory_space=pl.ANY),
        ],
        out_specs=(pl.BlockSpec(memory_space=pltpu.VMEM), pl.BlockSpec(memory_space=pl.ANY)),
        scratch_shapes=[
            pltpu.VMEM((FIELDS * ROWS, 512), BF16),
            pltpu.VMEM((2 * ROWS, 128), F32),
            pltpu.VMEM((DEVICES * SPAN, WIDTH), BF16),
            pltpu.SemaphoreType.DMA((2 * PIECES,)),
        ],
        compiler_params=pltpu.CompilerParams(vmem_limit_bytes=56 * 1024 * 1024),
        name="collect",
    )(back, slot, moved)


def exchange(x):
    return lax.all_to_all(x, AXES, split_axis=0, concat_axis=0, tiled=True)


def shards(file_fields, span_map, point_dest, point_local, point_coords):
    columns = jnp.arange(DEVICES, dtype=I32)
    inverse = jnp.zeros((DEVICES,), I32).at[span_map[0]].set(columns)
    pieces = file_fields.reshape(DEVICES, SPAN, WIDTH)[inverse]
    sent, slot = bucket(
        point_dest.reshape(1, POINTS), point_local.reshape(1, POINTS), point_coords
    )
    recv = exchange(sent.reshape(DEVICES, 8, 128))
    pieces, recv = lax.optimization_barrier((pieces, recv))
    moved = exchange(pieces).reshape(DEVICES * SPAN, WIDTH)
    values = evaluate(recv, span_map, file_fields)
    values, moved = lax.optimization_barrier((values, moved))
    back = exchange(values.reshape(DEVICES, 8, 128)).reshape(DEVICES // 2, 16, 128)
    return collect(back, slot, moved)


def solution(mesh):
    return jax.shard_map(
        shards,
        mesh=mesh,
        in_specs=(
            P(AXES, None),
            P(AXES, None),
            P(AXES, None),
            P(AXES),
            P(None, AXES),
        ),
        out_specs=(P(None, AXES), P(AXES, None)),
        check_vma=False,
    )
```

```python
import jax
import jax.numpy as jnp
import numpy as np
from jax import lax
from jax.experimental import pallas as pl
from jax.experimental.pallas import tpu as pltpu
from jax.sharding import PartitionSpec as P

NODES = 8
FIELDS = 5
SPAN = 8
DEVICES = 128
POINTS = 16384
CAP = 192
HALF = 64
WIDTH = FIELDS * NODES**3
SLOTS = DEVICES * CAP
GROUP = 64
GROUPS = 16
TILE = 256
ROWS = SLOTS // 256
MOST = SLOTS // TILE + GROUPS
AXES = ("owner", "sub")
F32 = jnp.float32
BF16 = jnp.bfloat16
I32 = jnp.int32


def gll_nodes(count):
    order = count - 1
    points = np.cos(np.pi * np.arange(count) / order)
    for sweep in range(100):
        oldest = np.ones(count)
        recent = points * 1.0
        for degree in range(2, order + 1):
            newest = ((2 * degree - 1) * points * recent - (degree - 1) * oldest) / degree
            oldest = recent
            recent = newest
        points = points - (points * recent - oldest) / (count * recent)
    return points[::-1]


def iota(shape, dim):
    return lax.broadcasted_iota(I32, shape, dim)


def lane_dot(a, b):
    return lax.dot_general(a, b, (((1,), (1,)), ((), ())), preferred_element_type=F32)


def dot(a, b):
    return jnp.dot(a, b, preferred_element_type=F32)


def parts(x):
    high = x.astype(BF16).astype(F32)
    return high, x - high


def earlier(rows, cols):
    return jnp.where(iota((rows, cols), 0) < iota((rows, cols), 1), 1.0, 0.0).astype(BF16)


def packed(value):
    return jnp.broadcast_to(value.astype(F32), (16, value.shape[1])).astype(BF16)


def onehot(first, rows, value):
    value = packed(value)
    base = iota(value.shape, 0)
    one, zero = jnp.asarray(1.0, BF16), jnp.asarray(0.0, BF16)
    out = []
    for r in range(rows // 16):
        out.append(jnp.where((base + (first + 16 * r)).astype(F32).astype(BF16) == value, one, zero))
    return jnp.concatenate(out, axis=0)


def spread(ones, value):
    value = packed(value)
    return jnp.concatenate(
        [ones[16 * r : 16 * r + 16] * value for r in range(ones.shape[0] // 16)], axis=0
    )


def both(ones, high, low):
    return jnp.concatenate([spread(ones, high), spread(ones, low)], axis=1)


def ranks(mask, before, base):
    ones = jnp.where(mask, 1.0, 0.0)
    narrow = ones.astype(BF16)
    counts = []
    for j in range(mask.shape[1] // 256):
        part = slice(256 * j, 256 * j + 256)
        inside = dot(narrow[:, part], before)
        counts.append(inside + base)
        base = base + inside[:, 255:256] + ones[:, 256 * j + 255 : 256 * j + 256]
    count = jnp.concatenate(counts, axis=1)
    return jnp.sum(jnp.where(mask, count, 0.0), axis=0, keepdims=True), base


def flat_slot(block, place):
    odd = (block & 1) == 1
    late = place >= 128
    return block * CAP + jnp.where(odd, jnp.where(late, place - 128, place + 64), place)


def to_grid(x):
    return ((x + 1.0) * 32767.5 + 0.5).astype(I32).astype(F32)


def from_grid(x):
    return x * (1.0 / 32767.5) - 1.0


def low_half(word):
    return (word << 16) >> 16


def high_half(word):
    return word >> 16


def left_halves(a, b):
    return jnp.where(iota(a.shape, 1) < HALF, a, pltpu.roll(b, HALF, 1))


def right_halves(a, b):
    return jnp.where(iota(a.shape, 1) < HALF, pltpu.roll(a, HALF, 1), b)


A_LANES = 4096


def bucket_kernel(
    dest_hbm, local_hbm, coords_hbm, out_ref, slot_ref, dest_ref, local_ref, coords_ref, acc_ref, flat_ref, sems
):
    copies = [
        pltpu.make_async_copy(src, dst, sems.at[n])
        for n, (src, dst) in enumerate(
            [(local_hbm, local_ref), (dest_hbm, dest_ref), (coords_hbm, coords_ref)]
        )
    ]
    for copy in copies:
        copy.start()
    acc_ref[...] = jnp.zeros_like(acc_ref)
    before = earlier(256, 256)
    steps = POINTS // A_LANES

    def at(n):
        return pl.ds(pl.multiple_of(n * A_LANES, A_LANES), A_LANES)

    def place(n, base):
        holder = local_ref[:, at(n)] >> 3
        rank, base = ranks(iota((DEVICES, A_LANES), 0) == holder, before, base)
        slot_ref[:, at(n)] = flat_slot(holder, rank.astype(I32))
        return base

    def scatter(n):
        slot = slot_ref[:, at(n)]
        where_row = onehot(0, ROWS, slot >> 8)
        where_col = onehot(0, 256, slot & 255)
        rows = [both(where_row, *parts(to_grid(coords_ref[k : k + 1, at(n)]))) for k in range(3)]
        rows.append(both(where_row, dest_ref[:, at(n)] * 8 + 8, local_ref[:, at(n)] & 7))
        wide = jnp.concatenate([where_col, where_col], axis=1)
        return lane_dot(jnp.concatenate(rows, axis=0), wide)

    copies[0].wait()
    base = place(0, jnp.zeros((DEVICES, 1), F32))
    copies[1].wait()
    copies[2].wait()

    def step(n, base):
        got = scatter(n)
        base = place(n + 1, base)
        acc_ref[...] += got
        return base

    lax.fori_loop(0, steps - 1, step, base)
    acc_ref[...] += scatter(steps - 1)
    middle = []
    for k in range(2):
        low, high = [
            acc_ref[q * ROWS : q * ROWS + ROWS, :].astype(I32) for q in (2 * k, 2 * k + 1)
        ]
        block = low + (high << 16)
        flat_ref[pl.ds(0, ROWS, 2), :] = block[:, 0:128]
        flat_ref[pl.ds(1, ROWS, 2), :] = block[:, 128:256]
        out_ref[:, k, :] = flat_ref[pl.ds(0, 64, 3), :]
        out_ref[:, 4 + k, :] = flat_ref[pl.ds(2, 64, 3), :]
        middle.append(flat_ref[pl.ds(1, 64, 3), :])
    out_ref[:, 2, :] = left_halves(*middle)
    out_ref[:, 6, :] = right_halves(*middle)
    out_ref[:, 3, :] = jnp.zeros((64, 128), I32)
    out_ref[:, 7, :] = jnp.zeros((64, 128), I32)


def bucket(dest, local, coords):
    return pl.pallas_call(
        bucket_kernel,
        out_shape=(
            jax.ShapeDtypeStruct((DEVICES // 2, 8, 128), I32),
            jax.ShapeDtypeStruct((1, POINTS), I32),
        ),
        in_specs=[pl.BlockSpec(memory_space=pl.ANY)] * 3,
        out_specs=(pl.BlockSpec(memory_space=pltpu.VMEM),) * 2,
        scratch_shapes=[
            pltpu.VMEM((1, POINTS), I32),
            pltpu.VMEM((1, POINTS), I32),
            pltpu.VMEM((3, POINTS), F32),
            pltpu.VMEM((4 * ROWS, 256), F32),
            pltpu.VMEM((2 * ROWS, 128), I32),
            pltpu.SemaphoreType.DMA((3,)),
        ],
        compiler_params=pltpu.CompilerParams(vmem_limit_bytes=56 * 1024 * 1024),
        name="bucket",
    )(dest, local, coords)


SOURCES = 16
C_LANES = SOURCES * CAP
STEPS = DEVICES // SOURCES
USUAL = 96
LEVELS = 32600.0
PAIR = 2
MANY = 8


def basis_rows(x, nodes, scale):
    row = iota((8, x.shape[1]), 0)
    out = None
    for n in range(8):
        term = jnp.where(row == n, scale, x - float(nodes[n]))
        out = term if out is None else out * term
    return out


def evaluate_kernel(
    recv_ref, span_ref, file_hbm, out_ref, file_ref, data_ref, sorted_ref, val_ref, acc_ref, flat_ref, first_ref, group_ref, sem
):
    load = pltpu.make_async_copy(file_hbm, file_ref, sem)
    load.start()
    nodes = gll_nodes(NODES)
    before = earlier(256, 256)
    permutation = jnp.where(iota((128, 128), 0) == span_ref[...], 1.0, 0.0).astype(BF16)
    inverse = lane_dot(iota((16, 128), 1).astype(F32).astype(BF16), permutation).astype(BF16)

    def count(n, base):
        blocks = [recv_ref[n * (SOURCES // 2) + s] for s in range(SOURCES // 2)]
        turned = [pltpu.roll(block, HALF, 1) for block in blocks]
        whole = jnp.concatenate(blocks, axis=1)
        swapped = jnp.concatenate(turned, axis=1)
        early = (iota((1, SOURCES * 64), 1) & 127) < HALF
        words = [
            jnp.concatenate(
                [whole[0:1], whole[4:5], jnp.where(early, whole[2:3], swapped[6:7])], axis=1
            ),
            jnp.concatenate(
                [whole[1:2], whole[5:6], jnp.where(early, swapped[2:3], whole[6:7])], axis=1
            ),
        ]
        number = high_half(words[1])
        span = dot(inverse, onehot(0, 128, (number >> 3) - 1))[0:1].astype(I32)
        group = jnp.where(number > 0, span >> 3, GROUPS)
        element = (span & 7) * 8 + (number & 7)
        rank, base = ranks(iota((GROUPS, C_LANES), 0) == group, before, base)
        lanes = pl.ds(pl.multiple_of(n * C_LANES, C_LANES), C_LANES)
        data_ref[0:1, lanes] = (words[0] & 0xFFFF).astype(F32)
        data_ref[1:2, lanes] = (high_half(words[0]) & 0xFFFF).astype(F32)
        data_ref[2:3, lanes] = (words[1] & 0xFFFF).astype(F32)
        data_ref[3:4, lanes] = element.astype(F32)
        data_ref[4:5, lanes] = group.astype(F32)
        data_ref[5:6, lanes] = rank
        return base

    total = lax.fori_loop(0, STEPS, count, jnp.zeros((GROUPS, 1), F32))
    tiles = ((total.astype(I32) + (TILE - 1)) >> 8).astype(F32)
    lower = jnp.where(iota((GROUPS, GROUPS), 1) < iota((GROUPS, GROUPS), 0), 1.0, 0.0)
    start = dot(lower.astype(BF16), jnp.broadcast_to(tiles, (GROUPS, 128)).astype(BF16))[:, 0:1]
    for g in range(GROUPS):
        first_ref[g] = jnp.sum(start[g : g + 1]).astype(I32)
    first_ref[GROUPS] = jnp.sum(tiles).astype(I32)
    used = first_ref[GROUPS]

    def name_group(g, carry):
        def name_tile(t, inner):
            group_ref[t] = g
            return inner

        return lax.fori_loop(first_ref[g], first_ref[g + 1], name_tile, carry)

    lax.fori_loop(0, GROUPS, name_group, 0)
    for n in range(PAIR - 1):
        group_ref[used + n] = 0

    sorted_ref[...] = jnp.zeros_like(sorted_ref)

    def sort(n, first, rows):
        lanes = pl.ds(pl.multiple_of(n * C_LANES, C_LANES), C_LANES)
        group = data_ref[4:5, lanes].astype(I32)
        here = iota((GROUPS, C_LANES), 0) == group
        base = jnp.sum(jnp.where(here, start, 0.0), axis=0, keepdims=True)
        slot = base.astype(I32) * TILE + data_ref[5:6, lanes].astype(I32)
        where_row = onehot(first, rows, jnp.where(group < GROUPS, slot >> 8, -1))
        where_col = onehot(0, TILE, slot & 255)
        at = iota((1, C_LANES), 1)
        pair = n * (SOURCES // 2) + ((at >> 7) & (SOURCES // 2 - 1))
        third = at >= SOURCES * 128
        odd = jnp.where(third, (at >> 6) & 1, jnp.where(at >= SOURCES * 64, 1, 0))
        back = flat_slot(2 * pair + odd, jnp.where(third, 128 + (at & 63), at & 127))
        lhs = [both(where_row, *parts(data_ref[k : k + 1, lanes])) for k in range(3)]
        lhs.append(both(where_row, ((back >> 8) + 1) * 64, data_ref[3:4, lanes]))
        wide = jnp.concatenate([where_col, where_col], axis=1)
        got = lane_dot(jnp.concatenate(lhs, axis=0), wide)
        last = lane_dot(spread(where_row, back & 255), where_col)
        for k in range(4):
            sorted_ref[k, first : first + rows, :] += got[k * rows : k * rows + rows]
        sorted_ref[4, first : first + rows, :] += last

    def usual(n, carry):
        sort(n, 0, USUAL)
        return carry

    lax.fori_loop(0, STEPS, usual, 0)

    @pl.when(used > USUAL)
    def _():
        def more(n, carry):
            sort(n, USUAL, MOST - USUAL)
            return carry

        lax.fori_loop(0, STEPS, more, 0)

    val_ref[...] = jnp.zeros_like(val_ref)
    load.wait()
    row8 = iota((8, TILE), 0)
    scales = jnp.zeros((8, TILE), F32)
    for i in range(8):
        value = 1.0
        for n in range(8):
            if n != i:
                value = value / (nodes[i] - nodes[n])
        scales = jnp.where(row8 == i, float(value), scales)

    def one_tile(t):
        rows = pl.ds(pl.multiple_of(group_ref[t] * GROUP, GROUP), GROUP)
        table = jnp.concatenate(
            [file_ref[rows, f * 512 : f * 512 + 512] for f in range(FIELDS)], axis=0
        )
        table = jnp.concatenate([table, table], axis=1)
        b0, b1, b2 = [basis_rows(from_grid(sorted_ref[k, pl.ds(t, 1), :]), nodes, scales) for k in range(3)]
        element = sorted_ref[3, pl.ds(t, 1), :].astype(I32) & 63
        planes = jnp.concatenate([b1[j : j + 1] * b2 for j in range(8)], axis=0)
        tops, lows = [], []
        for i in range(8):
            tensor = b0[i : i + 1] * planes
            top = tensor.astype(BF16)
            tops.append(top)
            lows.append((tensor - top.astype(F32)).astype(BF16))
        result = dot(table, jnp.concatenate(tops + lows, axis=0))
        mask = iota((GROUP, TILE), 0) == element
        return [
            jnp.sum(
                jnp.where(mask, result[f * GROUP : f * GROUP + GROUP], 0.0), axis=0, keepdims=True
            )
            for f in range(FIELDS)
        ]

    def on_tiles(n, carry):
        values = [one_tile(n * PAIR + q) for q in range(PAIR)]
        for q in range(PAIR):
            for f in range(FIELDS):
                val_ref[f, pl.ds(n * PAIR + q, 1), :] = values[q][f]
        return carry

    lax.fori_loop(0, (used + PAIR - 1) // PAIR, on_tiles, 0)

    acc_ref[...] = jnp.zeros_like(acc_ref)

    def back(n, carry):
        def row(ref, k):
            lines = [ref[k, pl.ds(n * MANY + q, 1), :] for q in range(MANY)]
            return jnp.concatenate(lines, axis=1)

        where_row = onehot(0, ROWS, (row(sorted_ref, 3).astype(I32) >> 6) - 1)
        where_col = onehot(0, 256, row(sorted_ref, 4))
        wide = jnp.concatenate([where_col, where_col], axis=1)
        lhs = [both(where_row, *parts(row(val_ref, f))) for f in range(FIELDS)]
        acc_ref[...] += lane_dot(jnp.concatenate(lhs, axis=0), wide)
        return carry

    lax.fori_loop(0, (used + MANY - 1) // MANY, back, 0)
    evens, odds, middle = [], [], []
    for f in range(FIELDS):
        block = acc_ref[f * ROWS : f * ROWS + ROWS, :]
        flat_ref[pl.ds(0, ROWS, 2), :] = block[:, 0:128]
        flat_ref[pl.ds(1, ROWS, 2), :] = block[:, 128:256]
        evens.append(flat_ref[pl.ds(0, 64, 3), :])
        odds.append(flat_ref[pl.ds(2, 64, 3), :])
        middle.append(flat_ref[pl.ds(1, 64, 3), :])
    low = iota((64, 128), 1) < HALF

    def exponent(firsts, own):
        most = jnp.zeros((64, 128), F32)
        for first, mid in zip(firsts, middle):
            most = jnp.maximum(most, jnp.abs(first))
            most = jnp.maximum(most, jnp.where(own, jnp.abs(mid), 0.0))
        most = jnp.max(most, axis=1, keepdims=True)
        power = jnp.ceil(jnp.log2(jnp.maximum(most, 1e-30)))
        return jnp.broadcast_to(power, (64, 128))

    def coded(value, factor):
        return jnp.floor(value * factor + 0.5).astype(I32)

    def word(a, b):
        return (a & 0xFFFF) | (b << 16)

    powers = [exponent(evens, low), exponent(odds, jnp.logical_not(low))]
    factors = [LEVELS * jnp.exp2(-power) for power in powers]
    last = [coded(mid, jnp.where(low, factors[0], factors[1])) for mid in middle]
    for odd, firsts in enumerate((evens, odds)):
        halves = right_halves if odd else left_halves
        first = [coded(value, factors[odd]) for value in firsts]
        power = powers[odd].astype(I32)
        out_ref[:, 4 * odd, :] = word(first[0], first[1])
        out_ref[:, 4 * odd + 1, :] = word(first[2], first[3])
        out_ref[:, 4 * odd + 2, :] = word(first[4], halves(last[0], last[1]))
        tail = pltpu.roll(last[3], HALF, 1) if odd else last[3]
        out_ref[:, 4 * odd + 3, :] = word(halves(last[2], last[4]), jnp.where(low, tail, power))


def evaluate(recv, span, file_fields):
    return pl.pallas_call(
        evaluate_kernel,
        out_shape=jax.ShapeDtypeStruct((DEVICES // 2, 8, 128), I32),
        in_specs=[
            pl.BlockSpec(memory_space=pltpu.VMEM),
            pl.BlockSpec(memory_space=pltpu.VMEM),
            pl.BlockSpec(memory_space=pl.ANY),
        ],
        out_specs=pl.BlockSpec(memory_space=pltpu.VMEM),
        scratch_shapes=[
            pltpu.VMEM((DEVICES * SPAN, WIDTH), BF16),
            pltpu.VMEM((8, SLOTS), F32),
            pltpu.VMEM((5, MOST, TILE), F32),
            pltpu.VMEM((FIELDS, MOST, TILE), F32),
            pltpu.VMEM((FIELDS * ROWS, 256), F32),
            pltpu.VMEM((2 * ROWS, 128), F32),
            pltpu.SMEM((GROUPS + 1,), I32),
            pltpu.SMEM((MOST + PAIR,), I32),
            pltpu.SemaphoreType.DMA(()),
        ],
        compiler_params=pltpu.CompilerParams(vmem_limit_bytes=56 * 1024 * 1024),
        cost_estimate=pl.CostEstimate(
            flops=60_000_000_000, bytes_accessed=6_000_000, transcendentals=0
        ),
        name="evaluate",
    )(recv, span, file_fields)


E_LANES = 2048
PIECES = 4


def collect_kernel(
    back_ref, slot_ref, moved_hbm, out_ref, owned_hbm, table_ref, flat_ref, held_ref, sems
):
    rows = DEVICES * SPAN // PIECES
    pieces = [pl.ds(n * rows, rows) for n in range(PIECES)]
    loads = [
        pltpu.make_async_copy(moved_hbm.at[p], held_ref.at[p], sems.at[n])
        for n, p in enumerate(pieces)
    ]
    stores = [
        pltpu.make_async_copy(held_ref.at[p], owned_hbm.at[p], sems.at[PIECES + n])
        for n, p in enumerate(pieces)
    ]
    for copy in loads:
        copy.start()
    firsts, lasts = [], []
    for odd in range(2):
        words = [back_ref[:, 4 * odd + r, :] for r in range(4)]
        tail = high_half(words[3])
        factor = jnp.exp2(right_halves(tail, tail).astype(F32)) * (1.0 / LEVELS)
        firsts.append(
            [
                half(words[r]).astype(F32) * factor
                for r, half in (
                    (0, low_half), (0, high_half), (1, low_half), (1, high_half), (2, low_half)
                )
            ]
        )
        lasts.append(
            [
                value.astype(F32) * factor
                for value in (high_half(words[2]), low_half(words[3]), tail)
            ]
        )
    for f in range(FIELDS):
        flat_ref[pl.ds(0, 64, 3), :] = firsts[0][f]
        flat_ref[pl.ds(2, 64, 3), :] = firsts[1][f]
        k, halves = ((0, left_halves), (0, right_halves), (1, left_halves), (2, left_halves), (1, right_halves))[f]
        flat_ref[pl.ds(1, 64, 3), :] = halves(lasts[0][k], lasts[1][k])
        for half in range(2):
            high, rest = parts(flat_ref[pl.ds(half, ROWS, 2), :])
            here = slice(f * ROWS, f * ROWS + ROWS)
            table_ref[here, 128 * half : 128 * half + 128] = high.astype(BF16)
            table_ref[here, 256 + 128 * half : 384 + 128 * half] = rest.astype(BF16)

    def step(n, carry):
        lanes = pl.ds(pl.multiple_of(n * E_LANES, E_LANES), E_LANES)
        slot = slot_ref[:, lanes]
        mask = iota((ROWS, E_LANES), 0) == (slot >> 8)
        where_col = onehot(0, 256, slot & 255)
        got = dot(table_ref[...], jnp.concatenate([where_col, where_col], axis=0))
        for f in range(FIELDS):
            out_ref[f : f + 1, lanes] = jnp.sum(
                jnp.where(mask, got[f * ROWS : f * ROWS + ROWS], 0.0), axis=0, keepdims=True
            )
        return carry

    steps = POINTS // E_LANES
    lax.fori_loop(0, steps // 2, step, 0, unroll=True)
    for load, store in zip(loads, stores):
        load.wait()
        store.start()
    lax.fori_loop(steps // 2, steps, step, 0, unroll=True)
    for store in stores:
        store.wait()


def collect(back, slot, moved):
    return pl.pallas_call(
        collect_kernel,
        out_shape=(
            jax.ShapeDtypeStruct((FIELDS, POINTS), F32),
            jax.ShapeDtypeStruct(moved.shape, moved.dtype),
        ),
        in_specs=[
            pl.BlockSpec(memory_space=pltpu.VMEM),
            pl.BlockSpec(memory_space=pltpu.VMEM),
            pl.BlockSpec(memory_space=pl.ANY),
        ],
        out_specs=(pl.BlockSpec(memory_space=pltpu.VMEM), pl.BlockSpec(memory_space=pl.ANY)),
        scratch_shapes=[
            pltpu.VMEM((FIELDS * ROWS, 512), BF16),
            pltpu.VMEM((2 * ROWS, 128), F32),
            pltpu.VMEM((DEVICES * SPAN, WIDTH), BF16),
            pltpu.SemaphoreType.DMA((2 * PIECES,)),
        ],
        compiler_params=pltpu.CompilerParams(vmem_limit_bytes=56 * 1024 * 1024),
        name="collect",
    )(back, slot, moved)


def exchange(x):
    return lax.all_to_all(x, AXES, split_axis=0, concat_axis=0, tiled=True)


def shards(file_fields, span_map, point_dest, point_local, point_coords):
    columns = jnp.arange(DEVICES, dtype=I32)
    inverse = jnp.zeros((DEVICES,), I32).at[span_map[0]].set(columns)
    pieces = file_fields.reshape(DEVICES, SPAN, WIDTH)[inverse]
    sent, slot = bucket(
        point_dest.reshape(1, POINTS), point_local.reshape(1, POINTS), point_coords
    )
    recv = exchange(sent.reshape(DEVICES, 4, 128)).reshape(DEVICES // 2, 8, 128)
    pieces, recv = lax.optimization_barrier((pieces, recv))
    moved = exchange(pieces).reshape(DEVICES * SPAN, WIDTH)
    values = evaluate(recv, span_map, file_fields)
    values, moved = lax.optimization_barrier((values, moved))
    back = exchange(values.reshape(DEVICES, 4, 128)).reshape(DEVICES // 2, 8, 128)
    return collect(back, slot, moved)


def solution(mesh):
    return jax.shard_map(
        shards,
        mesh=mesh,
        in_specs=(
            P(AXES, None),
            P(AXES, None),
            P(AXES, None),
            P(AXES),
            P(None, AXES),
        ),
        out_specs=(P(None, AXES), P(AXES, None)),
        check_vma=False,
    )
```

```python
import jax
import jax.numpy as jnp
import numpy as np
from jax import lax
from jax.experimental import pallas as pl
from jax.experimental.pallas import tpu as pltpu
from jax.sharding import PartitionSpec as P

NODES = 8
FIELDS = 5
SPAN = 8
DEVICES = 128
POINTS = 16384
CAP = 192
HALF = 64
WIDTH = FIELDS * NODES**3
SLOTS = DEVICES * CAP
GROUP = 64
GROUPS = 16
TILE = 256
ROWS = SLOTS // 256
MOST = SLOTS // TILE + GROUPS
AXES = ("owner", "sub")
F32 = jnp.float32
BF16 = jnp.bfloat16
I32 = jnp.int32


def gll_nodes(count):
    order = count - 1
    points = np.cos(np.pi * np.arange(count) / order)
    for sweep in range(100):
        oldest = np.ones(count)
        recent = points * 1.0
        for degree in range(2, order + 1):
            newest = ((2 * degree - 1) * points * recent - (degree - 1) * oldest) / degree
            oldest = recent
            recent = newest
        points = points - (points * recent - oldest) / (count * recent)
    return points[::-1]


def iota(shape, dim):
    return lax.broadcasted_iota(I32, shape, dim)


def lane_dot(a, b):
    return lax.dot_general(a, b, (((1,), (1,)), ((), ())), preferred_element_type=F32)


def dot(a, b):
    return jnp.dot(a, b, preferred_element_type=F32)


def parts(x):
    high = x.astype(BF16).astype(F32)
    return high, x - high


def earlier(rows, cols):
    return jnp.where(iota((rows, cols), 0) < iota((rows, cols), 1), 1.0, 0.0).astype(BF16)


def packed(value):
    return jnp.broadcast_to(value.astype(F32), (16, value.shape[1])).astype(BF16)


def onehot(first, rows, value):
    value = packed(value)
    base = iota(value.shape, 0)
    one, zero = jnp.asarray(1.0, BF16), jnp.asarray(0.0, BF16)
    out = []
    for r in range(rows // 16):
        out.append(jnp.where((base + (first + 16 * r)).astype(F32).astype(BF16) == value, one, zero))
    return jnp.concatenate(out, axis=0)


def spread(ones, value):
    value = packed(value)
    return jnp.concatenate(
        [ones[16 * r : 16 * r + 16] * value for r in range(ones.shape[0] // 16)], axis=0
    )


def both(ones, high, low):
    return jnp.concatenate([spread(ones, high), spread(ones, low)], axis=1)


def ranks(mask, before, base):
    ones = jnp.where(mask, 1.0, 0.0)
    narrow = ones.astype(BF16)
    counts = []
    for j in range(mask.shape[1] // 256):
        part = slice(256 * j, 256 * j + 256)
        inside = dot(narrow[:, part], before)
        counts.append(inside + base)
        base = base + inside[:, 255:256] + ones[:, 256 * j + 255 : 256 * j + 256]
    count = jnp.concatenate(counts, axis=1)
    return jnp.sum(jnp.where(mask, count, 0.0), axis=0, keepdims=True), base


def flat_slot(block, place):
    odd = (block & 1) == 1
    late = place >= 128
    return block * CAP + jnp.where(odd, jnp.where(late, place - 128, place + 64), place)


def to_grid(x):
    return ((x + 1.0) * 32767.5 + 0.5).astype(I32).astype(F32)


def from_grid(x):
    return x * (1.0 / 32767.5) - 1.0


def low_half(word):
    return (word << 16) >> 16


def high_half(word):
    return word >> 16


def left_halves(a, b):
    return jnp.where(iota(a.shape, 1) < HALF, a, pltpu.roll(b, HALF, 1))


def right_halves(a, b):
    return jnp.where(iota(a.shape, 1) < HALF, pltpu.roll(a, HALF, 1), b)


A_LANES = 4096


def bucket_kernel(
    dest_hbm, local_hbm, coords_hbm, out_ref, slot_ref, dest_ref, local_ref, coords_ref, acc_ref, flat_ref, sems
):
    copies = [
        pltpu.make_async_copy(src, dst, sems.at[n])
        for n, (src, dst) in enumerate(
            [(local_hbm, local_ref), (dest_hbm, dest_ref), (coords_hbm, coords_ref)]
        )
    ]
    for copy in copies:
        copy.start()
    acc_ref[...] = jnp.zeros_like(acc_ref)
    before = earlier(256, 256)
    steps = POINTS // A_LANES

    def at(n):
        return pl.ds(pl.multiple_of(n * A_LANES, A_LANES), A_LANES)

    def place(n, base):
        holder = local_ref[:, at(n)] >> 3
        rank, base = ranks(iota((DEVICES, A_LANES), 0) == holder, before, base)
        slot_ref[:, at(n)] = flat_slot(holder, rank.astype(I32))
        return base

    def scatter(n):
        slot = slot_ref[:, at(n)]
        where_row = onehot(0, ROWS, slot >> 8)
        where_col = onehot(0, 256, slot & 255)
        rows = [both(where_row, *parts(to_grid(coords_ref[k : k + 1, at(n)]))) for k in range(3)]
        rows.append(both(where_row, dest_ref[:, at(n)] * 8 + 8, local_ref[:, at(n)] & 7))
        wide = jnp.concatenate([where_col, where_col], axis=1)
        return lane_dot(jnp.concatenate(rows, axis=0), wide)

    copies[0].wait()
    base = place(0, jnp.zeros((DEVICES, 1), F32))
    copies[1].wait()
    copies[2].wait()

    def step(n, base):
        got = scatter(n)
        base = place(n + 1, base)
        acc_ref[...] += got
        return base

    lax.fori_loop(0, steps - 1, step, base)
    acc_ref[...] += scatter(steps - 1)
    middle = []
    for k in range(2):
        low, high = [
            acc_ref[q * ROWS : q * ROWS + ROWS, :].astype(I32) for q in (2 * k, 2 * k + 1)
        ]
        block = low + (high << 16)
        flat_ref[pl.ds(0, ROWS, 2), :] = block[:, 0:128]
        flat_ref[pl.ds(1, ROWS, 2), :] = block[:, 128:256]
        out_ref[:, k, :] = flat_ref[pl.ds(0, 64, 3), :]
        out_ref[:, 4 + k, :] = flat_ref[pl.ds(2, 64, 3), :]
        middle.append(flat_ref[pl.ds(1, 64, 3), :])
    out_ref[:, 2, :] = left_halves(*middle)
    out_ref[:, 6, :] = right_halves(*middle)
    out_ref[:, 3, :] = jnp.zeros((64, 128), I32)
    out_ref[:, 7, :] = jnp.zeros((64, 128), I32)


def bucket(dest, local, coords):
    return pl.pallas_call(
        bucket_kernel,
        out_shape=(
            jax.ShapeDtypeStruct((DEVICES // 2, 8, 128), I32),
            jax.ShapeDtypeStruct((1, POINTS), I32),
        ),
        in_specs=[pl.BlockSpec(memory_space=pl.ANY)] * 3,
        out_specs=(pl.BlockSpec(memory_space=pltpu.VMEM),) * 2,
        scratch_shapes=[
            pltpu.VMEM((1, POINTS), I32),
            pltpu.VMEM((1, POINTS), I32),
            pltpu.VMEM((3, POINTS), F32),
            pltpu.VMEM((4 * ROWS, 256), F32),
            pltpu.VMEM((2 * ROWS, 128), I32),
            pltpu.SemaphoreType.DMA((3,)),
        ],
        compiler_params=pltpu.CompilerParams(vmem_limit_bytes=56 * 1024 * 1024),
        name="bucket",
    )(dest, local, coords)


SOURCES = 32
C_LANES = SOURCES * CAP
STEPS = DEVICES // SOURCES
USUAL = 96
LEVELS = 32600.0
PAIR = 8
MANY = 16


def basis_rows(x, nodes, scale):
    row = iota((8, x.shape[1]), 0)
    out = None
    for n in range(8):
        term = jnp.where(row == n, scale, x - float(nodes[n]))
        out = term if out is None else out * term
    return out


def evaluate_kernel(
    recv_ref, span_ref, file_hbm, out_ref, file_ref, data_ref, sorted_ref, val_ref, acc_ref, flat_ref, first_ref, group_ref, sem
):
    load = pltpu.make_async_copy(file_hbm, file_ref, sem)
    load.start()
    nodes = gll_nodes(NODES)
    before = earlier(256, 256)
    permutation = jnp.where(iota((128, 128), 0) == span_ref[...], 1.0, 0.0).astype(BF16)
    inverse = lane_dot(iota((16, 128), 1).astype(F32).astype(BF16), permutation).astype(BF16)

    def count(n, base):
        blocks = [recv_ref[n * (SOURCES // 2) + s] for s in range(SOURCES // 2)]
        turned = [pltpu.roll(block, HALF, 1) for block in blocks]
        whole = jnp.concatenate(blocks, axis=1)
        swapped = jnp.concatenate(turned, axis=1)
        early = (iota((1, SOURCES * 64), 1) & 127) < HALF
        words = [
            jnp.concatenate(
                [whole[0:1], whole[4:5], jnp.where(early, whole[2:3], swapped[6:7])], axis=1
            ),
            jnp.concatenate(
                [whole[1:2], whole[5:6], jnp.where(early, swapped[2:3], whole[6:7])], axis=1
            ),
        ]
        number = high_half(words[1])
        span = dot(inverse, onehot(0, 128, (number >> 3) - 1))[0:1].astype(I32)
        group = jnp.where(number > 0, span >> 3, GROUPS)
        element = (span & 7) * 8 + (number & 7)
        rank, base = ranks(iota((GROUPS, C_LANES), 0) == group, before, base)
        lanes = pl.ds(pl.multiple_of(n * C_LANES, C_LANES), C_LANES)
        data_ref[0:1, lanes] = (words[0] & 0xFFFF).astype(F32)
        data_ref[1:2, lanes] = (high_half(words[0]) & 0xFFFF).astype(F32)
        data_ref[2:3, lanes] = (words[1] & 0xFFFF).astype(F32)
        data_ref[3:4, lanes] = element.astype(F32)
        data_ref[4:5, lanes] = group.astype(F32)
        data_ref[5:6, lanes] = rank
        return base

    total = lax.fori_loop(0, STEPS, count, jnp.zeros((GROUPS, 1), F32))
    tiles = ((total.astype(I32) + (TILE - 1)) >> 8).astype(F32)
    lower = jnp.where(iota((GROUPS, GROUPS), 1) < iota((GROUPS, GROUPS), 0), 1.0, 0.0)
    start = dot(lower.astype(BF16), jnp.broadcast_to(tiles, (GROUPS, 128)).astype(BF16))[:, 0:1]
    for g in range(GROUPS):
        first_ref[g] = jnp.sum(start[g : g + 1]).astype(I32)
    first_ref[GROUPS] = jnp.sum(tiles).astype(I32)
    used = first_ref[GROUPS]

    def name_group(g, carry):
        def name_tile(t, inner):
            group_ref[t] = g
            return inner

        return lax.fori_loop(first_ref[g], first_ref[g + 1], name_tile, carry)

    lax.fori_loop(0, GROUPS, name_group, 0)
    for n in range(PAIR - 1):
        group_ref[used + n] = 0

    sorted_ref[...] = jnp.zeros_like(sorted_ref)

    def sort(n, first, rows):
        lanes = pl.ds(pl.multiple_of(n * C_LANES, C_LANES), C_LANES)
        group = data_ref[4:5, lanes].astype(I32)
        here = iota((GROUPS, C_LANES), 0) == group
        base = jnp.sum(jnp.where(here, start, 0.0), axis=0, keepdims=True)
        slot = base.astype(I32) * TILE + data_ref[5:6, lanes].astype(I32)
        where_row = onehot(first, rows, jnp.where(group < GROUPS, slot >> 8, -1))
        where_col = onehot(0, TILE, slot & 255)
        at = iota((1, C_LANES), 1)
        pair = n * (SOURCES // 2) + ((at >> 7) & (SOURCES // 2 - 1))
        third = at >= SOURCES * 128
        odd = jnp.where(third, (at >> 6) & 1, jnp.where(at >= SOURCES * 64, 1, 0))
        back = flat_slot(2 * pair + odd, jnp.where(third, 128 + (at & 63), at & 127))
        lhs = [both(where_row, *parts(data_ref[k : k + 1, lanes])) for k in range(3)]
        lhs.append(both(where_row, ((back >> 8) + 1) * 64, data_ref[3:4, lanes]))
        wide = jnp.concatenate([where_col, where_col], axis=1)
        got = lane_dot(jnp.concatenate(lhs, axis=0), wide)
        last = lane_dot(spread(where_row, back & 255), where_col)
        for k in range(4):
            sorted_ref[k, first : first + rows, :] += got[k * rows : k * rows + rows]
        sorted_ref[4, first : first + rows, :] += last

    def usual(n, carry):
        sort(n, 0, USUAL)
        return carry

    lax.fori_loop(0, STEPS, usual, 0)

    @pl.when(used > USUAL)
    def _():
        def more(n, carry):
            sort(n, USUAL, MOST - USUAL)
            return carry

        lax.fori_loop(0, STEPS, more, 0)

    val_ref[...] = jnp.zeros_like(val_ref)
    load.wait()
    row8 = iota((8, TILE), 0)
    scales = jnp.zeros((8, TILE), F32)
    for i in range(8):
        value = 1.0
        for n in range(8):
            if n != i:
                value = value / (nodes[i] - nodes[n])
        scales = jnp.where(row8 == i, float(value), scales)

    def one_tile(t):
        rows = pl.ds(pl.multiple_of(group_ref[t] * GROUP, GROUP), GROUP)
        table = jnp.concatenate(
            [file_ref[rows, f * 512 : f * 512 + 512] for f in range(FIELDS)], axis=0
        )
        table = jnp.concatenate([table, table], axis=1)
        b0, b1, b2 = [basis_rows(from_grid(sorted_ref[k, pl.ds(t, 1), :]), nodes, scales) for k in range(3)]
        element = sorted_ref[3, pl.ds(t, 1), :].astype(I32) & 63
        planes = jnp.concatenate([b1[j : j + 1] * b2 for j in range(8)], axis=0)
        tops, lows = [], []
        for i in range(8):
            tensor = b0[i : i + 1] * planes
            top = tensor.astype(BF16)
            tops.append(top)
            lows.append((tensor - top.astype(F32)).astype(BF16))
        result = dot(table, jnp.concatenate(tops + lows, axis=0))
        mask = iota((GROUP, TILE), 0) == element
        return [
            jnp.sum(
                jnp.where(mask, result[f * GROUP : f * GROUP + GROUP], 0.0), axis=0, keepdims=True
            )
            for f in range(FIELDS)
        ]

    def on_tiles(n, carry):
        values = [one_tile(n * PAIR + q) for q in range(PAIR)]
        for q in range(PAIR):
            for f in range(FIELDS):
                val_ref[f, pl.ds(n * PAIR + q, 1), :] = values[q][f]
        return carry

    lax.fori_loop(0, (used + PAIR - 1) // PAIR, on_tiles, 0)

    acc_ref[...] = jnp.zeros_like(acc_ref)

    def back(n, carry):
        def row(ref, k):
            lines = [ref[k, pl.ds(n * MANY + q, 1), :] for q in range(MANY)]
            return jnp.concatenate(lines, axis=1)

        where_row = onehot(0, ROWS, (row(sorted_ref, 3).astype(I32) >> 6) - 1)
        where_col = onehot(0, 256, row(sorted_ref, 4))
        wide = jnp.concatenate([where_col, where_col], axis=1)
        lhs = [both(where_row, *parts(row(val_ref, f))) for f in range(FIELDS)]
        acc_ref[...] += lane_dot(jnp.concatenate(lhs, axis=0), wide)
        return carry

    lax.fori_loop(0, (used + MANY - 1) // MANY, back, 0)
    evens, odds, middle = [], [], []
    for f in range(FIELDS):
        block = acc_ref[f * ROWS : f * ROWS + ROWS, :]
        flat_ref[pl.ds(0, ROWS, 2), :] = block[:, 0:128]
        flat_ref[pl.ds(1, ROWS, 2), :] = block[:, 128:256]
        evens.append(flat_ref[pl.ds(0, 64, 3), :])
        odds.append(flat_ref[pl.ds(2, 64, 3), :])
        middle.append(flat_ref[pl.ds(1, 64, 3), :])
    low = iota((64, 128), 1) < HALF

    def exponent(firsts, own):
        most = jnp.zeros((64, 128), F32)
        for first, mid in zip(firsts, middle):
            most = jnp.maximum(most, jnp.abs(first))
            most = jnp.maximum(most, jnp.where(own, jnp.abs(mid), 0.0))
        most = jnp.max(most, axis=1, keepdims=True)
        power = jnp.ceil(jnp.log2(jnp.maximum(most, 1e-30)))
        return jnp.broadcast_to(power, (64, 128))

    def coded(value, factor):
        return jnp.floor(value * factor + 0.5).astype(I32)

    def word(a, b):
        return (a & 0xFFFF) | (b << 16)

    powers = [exponent(evens, low), exponent(odds, jnp.logical_not(low))]
    factors = [LEVELS * jnp.exp2(-power) for power in powers]
    last = [coded(mid, jnp.where(low, factors[0], factors[1])) for mid in middle]
    for odd, firsts in enumerate((evens, odds)):
        halves = right_halves if odd else left_halves
        first = [coded(value, factors[odd]) for value in firsts]
        power = powers[odd].astype(I32)
        out_ref[:, 4 * odd, :] = word(first[0], first[1])
        out_ref[:, 4 * odd + 1, :] = word(first[2], first[3])
        out_ref[:, 4 * odd + 2, :] = word(first[4], halves(last[0], last[1]))
        tail = pltpu.roll(last[3], HALF, 1) if odd else last[3]
        out_ref[:, 4 * odd + 3, :] = word(halves(last[2], last[4]), jnp.where(low, tail, power))


def evaluate(recv, span, file_fields):
    return pl.pallas_call(
        evaluate_kernel,
        out_shape=jax.ShapeDtypeStruct((DEVICES // 2, 8, 128), I32),
        in_specs=[
            pl.BlockSpec(memory_space=pltpu.VMEM),
            pl.BlockSpec(memory_space=pltpu.VMEM),
            pl.BlockSpec(memory_space=pl.ANY),
        ],
        out_specs=pl.BlockSpec(memory_space=pltpu.VMEM),
        scratch_shapes=[
            pltpu.VMEM((DEVICES * SPAN, WIDTH), BF16),
            pltpu.VMEM((8, SLOTS), F32),
            pltpu.VMEM((5, MOST, TILE), F32),
            pltpu.VMEM((FIELDS, MOST, TILE), F32),
            pltpu.VMEM((FIELDS * ROWS, 256), F32),
            pltpu.VMEM((2 * ROWS, 128), F32),
            pltpu.SMEM((GROUPS + 1,), I32),
            pltpu.SMEM((MOST + PAIR,), I32),
            pltpu.SemaphoreType.DMA(()),
        ],
        compiler_params=pltpu.CompilerParams(vmem_limit_bytes=56 * 1024 * 1024),
        cost_estimate=pl.CostEstimate(
            flops=60_000_000_000, bytes_accessed=6_000_000, transcendentals=0
        ),
        name="evaluate",
    )(recv, span, file_fields)


E_LANES = 2048
PIECES = 4


def collect_kernel(
    back_ref, slot_ref, moved_hbm, out_ref, owned_hbm, table_ref, flat_ref, held_ref, sems
):
    rows = DEVICES * SPAN // PIECES
    pieces = [pl.ds(n * rows, rows) for n in range(PIECES)]
    loads = [
        pltpu.make_async_copy(moved_hbm.at[p], held_ref.at[p], sems.at[n])
        for n, p in enumerate(pieces)
    ]
    stores = [
        pltpu.make_async_copy(held_ref.at[p], owned_hbm.at[p], sems.at[PIECES + n])
        for n, p in enumerate(pieces)
    ]
    for copy in loads:
        copy.start()
    firsts, lasts = [], []
    for odd in range(2):
        words = [back_ref[:, 4 * odd + r, :] for r in range(4)]
        tail = high_half(words[3])
        factor = jnp.exp2(right_halves(tail, tail).astype(F32)) * (1.0 / LEVELS)
        firsts.append(
            [
                half(words[r]).astype(F32) * factor
                for r, half in (
                    (0, low_half), (0, high_half), (1, low_half), (1, high_half), (2, low_half)
                )
            ]
        )
        lasts.append(
            [
                value.astype(F32) * factor
                for value in (high_half(words[2]), low_half(words[3]), tail)
            ]
        )
    for f in range(FIELDS):
        flat_ref[pl.ds(0, 64, 3), :] = firsts[0][f]
        flat_ref[pl.ds(2, 64, 3), :] = firsts[1][f]
        k, halves = ((0, left_halves), (0, right_halves), (1, left_halves), (2, left_halves), (1, right_halves))[f]
        flat_ref[pl.ds(1, 64, 3), :] = halves(lasts[0][k], lasts[1][k])
        for half in range(2):
            high, rest = parts(flat_ref[pl.ds(half, ROWS, 2), :])
            here = slice(f * ROWS, f * ROWS + ROWS)
            table_ref[here, 128 * half : 128 * half + 128] = high.astype(BF16)
            table_ref[here, 256 + 128 * half : 384 + 128 * half] = rest.astype(BF16)

    def step(n, carry):
        lanes = pl.ds(pl.multiple_of(n * E_LANES, E_LANES), E_LANES)
        slot = slot_ref[:, lanes]
        mask = iota((ROWS, E_LANES), 0) == (slot >> 8)
        where_col = onehot(0, 256, slot & 255)
        got = dot(table_ref[...], jnp.concatenate([where_col, where_col], axis=0))
        for f in range(FIELDS):
            out_ref[f : f + 1, lanes] = jnp.sum(
                jnp.where(mask, got[f * ROWS : f * ROWS + ROWS], 0.0), axis=0, keepdims=True
            )
        return carry

    steps = POINTS // E_LANES
    lax.fori_loop(0, steps // 2, step, 0, unroll=True)
    for load, store in zip(loads, stores):
        load.wait()
        store.start()
    lax.fori_loop(steps // 2, steps, step, 0, unroll=True)
    for store in stores:
        store.wait()


def collect(back, slot, moved):
    return pl.pallas_call(
        collect_kernel,
        out_shape=(
            jax.ShapeDtypeStruct((FIELDS, POINTS), F32),
            jax.ShapeDtypeStruct(moved.shape, moved.dtype),
        ),
        in_specs=[
            pl.BlockSpec(memory_space=pltpu.VMEM),
            pl.BlockSpec(memory_space=pltpu.VMEM),
            pl.BlockSpec(memory_space=pl.ANY),
        ],
        out_specs=(pl.BlockSpec(memory_space=pltpu.VMEM), pl.BlockSpec(memory_space=pl.ANY)),
        scratch_shapes=[
            pltpu.VMEM((FIELDS * ROWS, 512), BF16),
            pltpu.VMEM((2 * ROWS, 128), F32),
            pltpu.VMEM((DEVICES * SPAN, WIDTH), BF16),
            pltpu.SemaphoreType.DMA((2 * PIECES,)),
        ],
        compiler_params=pltpu.CompilerParams(vmem_limit_bytes=56 * 1024 * 1024),
        name="collect",
    )(back, slot, moved)


def exchange(x):
    return lax.all_to_all(x, AXES, split_axis=0, concat_axis=0, tiled=True)


def shards(file_fields, span_map, point_dest, point_local, point_coords):
    columns = jnp.arange(DEVICES, dtype=I32)
    inverse = jnp.zeros((DEVICES,), I32).at[span_map[0]].set(columns)
    pieces = file_fields.reshape(DEVICES, SPAN, WIDTH)[inverse]
    sent, slot = bucket(
        point_dest.reshape(1, POINTS), point_local.reshape(1, POINTS), point_coords
    )
    recv = exchange(sent.reshape(DEVICES, 4, 128)).reshape(DEVICES // 2, 8, 128)
    pieces, recv = lax.optimization_barrier((pieces, recv))
    moved = exchange(pieces).reshape(DEVICES * SPAN, WIDTH)
    values = evaluate(recv, span_map, file_fields)
    values, moved = lax.optimization_barrier((values, moved))
    back = exchange(values.reshape(DEVICES, 4, 128)).reshape(DEVICES // 2, 8, 128)
    return collect(back, slot, moved)


def solution(mesh):
    return jax.shard_map(
        shards,
        mesh=mesh,
        in_specs=(
            P(AXES, None),
            P(AXES, None),
            P(AXES, None),
            P(AXES),
            P(None, AXES),
        ),
        out_specs=(P(None, AXES), P(AXES, None)),
        check_vma=False,
    )
```

```python
import jax
import jax.numpy as jnp
import numpy as np
from jax import lax
from jax.experimental import pallas as pl
from jax.experimental.pallas import tpu as pltpu
from jax.sharding import PartitionSpec as P

NODES = 8
FIELDS = 5
SPAN = 8
DEVICES = 128
POINTS = 16384
CAP = 192
HALF = 64
WIDTH = FIELDS * NODES**3
SLOTS = DEVICES * CAP
GROUP = 64
GROUPS = 16
TILE = 256
ROWS = SLOTS // 256
MOST = SLOTS // TILE + GROUPS
AXES = ("owner", "sub")
F32 = jnp.float32
BF16 = jnp.bfloat16
I32 = jnp.int32


def gll_nodes(count):
    order = count - 1
    points = np.cos(np.pi * np.arange(count) / order)
    for sweep in range(100):
        oldest = np.ones(count)
        recent = points * 1.0
        for degree in range(2, order + 1):
            newest = ((2 * degree - 1) * points * recent - (degree - 1) * oldest) / degree
            oldest = recent
            recent = newest
        points = points - (points * recent - oldest) / (count * recent)
    return points[::-1]


def iota(shape, dim):
    return lax.broadcasted_iota(I32, shape, dim)


def lane_dot(a, b):
    return lax.dot_general(a, b, (((1,), (1,)), ((), ())), preferred_element_type=F32)


def dot(a, b):
    return jnp.dot(a, b, preferred_element_type=F32)


def parts(x):
    high = x.astype(BF16).astype(F32)
    return high, x - high


def earlier(rows, cols):
    return jnp.where(iota((rows, cols), 0) < iota((rows, cols), 1), 1.0, 0.0).astype(BF16)


def packed(value):
    return jnp.broadcast_to(value.astype(F32), (16, value.shape[1])).astype(BF16)


def onehot(first, rows, value):
    value = packed(value)
    base = iota(value.shape, 0)
    one, zero = jnp.asarray(1.0, BF16), jnp.asarray(0.0, BF16)
    out = []
    for r in range(rows // 16):
        out.append(jnp.where((base + (first + 16 * r)).astype(F32).astype(BF16) == value, one, zero))
    return jnp.concatenate(out, axis=0)


def spread(ones, value):
    value = packed(value)
    return jnp.concatenate(
        [ones[16 * r : 16 * r + 16] * value for r in range(ones.shape[0] // 16)], axis=0
    )


def both(ones, high, low):
    return jnp.concatenate([spread(ones, high), spread(ones, low)], axis=1)


def ranks(mask, before, base):
    ones = jnp.where(mask, 1.0, 0.0)
    narrow = ones.astype(BF16)
    counts = []
    rows, blocks = mask.shape[0], mask.shape[1] // 256
    stacked = [narrow[:, 256 * j : 256 * j + 256] for j in range(blocks)]
    stacked = dot(jnp.concatenate(stacked, axis=0), before)
    for j in range(blocks):
        inside = stacked[rows * j : rows * j + rows]
        counts.append(inside + base)
        base = base + inside[:, 255:256] + ones[:, 256 * j + 255 : 256 * j + 256]
    count = jnp.concatenate(counts, axis=1)
    return jnp.sum(jnp.where(mask, count, 0.0), axis=0, keepdims=True), base


def flat_slot(block, place):
    odd = (block & 1) == 1
    late = place >= 128
    return block * CAP + jnp.where(odd, jnp.where(late, place - 128, place + 64), place)


def to_grid(x):
    return ((x + 1.0) * 32767.5 + 0.5).astype(I32).astype(F32)


def from_grid(x):
    return x * (1.0 / 32767.5) - 1.0


def low_half(word):
    return (word << 16) >> 16


def high_half(word):
    return word >> 16


def left_halves(a, b):
    return jnp.where(iota(a.shape, 1) < HALF, a, pltpu.roll(b, HALF, 1))


def right_halves(a, b):
    return jnp.where(iota(a.shape, 1) < HALF, pltpu.roll(a, HALF, 1), b)


A_LANES = 4096


def bucket_kernel(
    dest_hbm, local_hbm, coords_hbm, out_ref, slot_ref, dest_ref, local_ref, coords_ref, acc_ref, flat_ref, sems
):
    early, late = pl.ds(0, A_LANES), pl.ds(A_LANES, POINTS - A_LANES)
    copies = [
        pltpu.make_async_copy(src, dst, sems.at[n])
        for n, (src, dst) in enumerate(
            [
                (local_hbm.at[:, early], local_ref.at[:, early]),
                (local_hbm.at[:, late], local_ref.at[:, late]),
                (dest_hbm, dest_ref),
                (coords_hbm, coords_ref),
            ]
        )
    ]
    for copy in copies:
        copy.start()
    acc_ref[...] = jnp.zeros_like(acc_ref)
    before = earlier(256, 256)
    steps = POINTS // A_LANES

    def at(n):
        return pl.ds(pl.multiple_of(n * A_LANES, A_LANES), A_LANES)

    def place(n, base):
        holder = local_ref[:, at(n)] >> 3
        rank, base = ranks(iota((DEVICES, A_LANES), 0) == holder, before, base)
        slot_ref[:, at(n)] = flat_slot(holder, rank.astype(I32))
        return base

    def scatter(n):
        slot = slot_ref[:, at(n)]
        where_row = onehot(0, ROWS, slot >> 8)
        where_col = onehot(0, 256, slot & 255)
        rows = [both(where_row, *parts(to_grid(coords_ref[k : k + 1, at(n)]))) for k in range(3)]
        rows.append(both(where_row, dest_ref[:, at(n)] * 8 + 8, local_ref[:, at(n)] & 7))
        wide = jnp.concatenate([where_col, where_col], axis=1)
        return lane_dot(jnp.concatenate(rows, axis=0), wide)

    copies[0].wait()
    base = place(0, jnp.zeros((DEVICES, 1), F32))
    for copy in copies[1:]:
        copy.wait()

    def step(n, base):
        got = scatter(n)
        base = place(n + 1, base)
        acc_ref[...] += got
        return base

    lax.fori_loop(0, steps - 1, step, base)
    acc_ref[...] += scatter(steps - 1)
    middle = []
    for k in range(2):
        low, high = [
            acc_ref[q * ROWS : q * ROWS + ROWS, :].astype(I32) for q in (2 * k, 2 * k + 1)
        ]
        block = low + (high << 16)
        flat_ref[pl.ds(0, ROWS, 2), :] = block[:, 0:128]
        flat_ref[pl.ds(1, ROWS, 2), :] = block[:, 128:256]
        out_ref[:, k, :] = flat_ref[pl.ds(0, 64, 3), :]
        out_ref[:, 4 + k, :] = flat_ref[pl.ds(2, 64, 3), :]
        middle.append(flat_ref[pl.ds(1, 64, 3), :])
    out_ref[:, 2, :] = left_halves(*middle)
    out_ref[:, 6, :] = right_halves(*middle)
    out_ref[:, 3, :] = jnp.zeros((64, 128), I32)
    out_ref[:, 7, :] = jnp.zeros((64, 128), I32)


def bucket(dest, local, coords):
    return pl.pallas_call(
        bucket_kernel,
        out_shape=(
            jax.ShapeDtypeStruct((DEVICES // 2, 8, 128), I32),
            jax.ShapeDtypeStruct((1, POINTS), I32),
        ),
        in_specs=[pl.BlockSpec(memory_space=pl.ANY)] * 3,
        out_specs=(pl.BlockSpec(memory_space=pltpu.VMEM),) * 2,
        scratch_shapes=[
            pltpu.VMEM((1, POINTS), I32),
            pltpu.VMEM((1, POINTS), I32),
            pltpu.VMEM((3, POINTS), F32),
            pltpu.VMEM((4 * ROWS, 256), F32),
            pltpu.VMEM((2 * ROWS, 128), I32),
            pltpu.SemaphoreType.DMA((4,)),
        ],
        compiler_params=pltpu.CompilerParams(vmem_limit_bytes=56 * 1024 * 1024),
        name="bucket",
    )(dest, local, coords)


SOURCES = 32
C_LANES = SOURCES * CAP
STEPS = DEVICES // SOURCES
USUAL = 96
LEVELS = 32600.0
PAIR = 8
MANY = 16


def basis_rows(x, nodes, scale):
    row = iota((8, x.shape[1]), 0)
    out = None
    for n in range(8):
        term = jnp.where(row == n, scale, x - float(nodes[n]))
        out = term if out is None else out * term
    return out


def evaluate_kernel(
    recv_ref, span_ref, file_hbm, out_ref, file_ref, data_ref, sorted_ref, val_ref, acc_ref, flat_ref, first_ref, group_ref, sem
):
    load = pltpu.make_async_copy(file_hbm, file_ref, sem)
    load.start()
    nodes = gll_nodes(NODES)
    before = earlier(256, 256)
    permutation = jnp.where(iota((128, 128), 0) == span_ref[...], 1.0, 0.0).astype(BF16)
    inverse = lane_dot(iota((16, 128), 1).astype(F32).astype(BF16), permutation).astype(BF16)

    def count(n, base):
        blocks = [recv_ref[n * (SOURCES // 2) + s] for s in range(SOURCES // 2)]
        turned = [pltpu.roll(block, HALF, 1) for block in blocks]
        whole = jnp.concatenate(blocks, axis=1)
        swapped = jnp.concatenate(turned, axis=1)
        early = (iota((1, SOURCES * 64), 1) & 127) < HALF
        words = [
            jnp.concatenate(
                [whole[0:1], whole[4:5], jnp.where(early, whole[2:3], swapped[6:7])], axis=1
            ),
            jnp.concatenate(
                [whole[1:2], whole[5:6], jnp.where(early, swapped[2:3], whole[6:7])], axis=1
            ),
        ]
        number = high_half(words[1])
        span = dot(inverse, onehot(0, 128, (number >> 3) - 1))[0:1].astype(I32)
        group = jnp.where(number > 0, span >> 3, GROUPS)
        element = (span & 7) * 8 + (number & 7)
        rank, base = ranks(iota((GROUPS, C_LANES), 0) == group, before, base)
        lanes = pl.ds(pl.multiple_of(n * C_LANES, C_LANES), C_LANES)
        data_ref[0:1, lanes] = (words[0] & 0xFFFF).astype(F32)
        data_ref[1:2, lanes] = (high_half(words[0]) & 0xFFFF).astype(F32)
        data_ref[2:3, lanes] = (words[1] & 0xFFFF).astype(F32)
        data_ref[3:4, lanes] = element.astype(F32)
        data_ref[4:5, lanes] = group.astype(F32)
        data_ref[5:6, lanes] = rank
        return base

    total = lax.fori_loop(0, STEPS, count, jnp.zeros((GROUPS, 1), F32))
    tiles = ((total.astype(I32) + (TILE - 1)) >> 8).astype(F32)
    lower = jnp.where(iota((GROUPS, GROUPS), 1) < iota((GROUPS, GROUPS), 0), 1.0, 0.0)
    start = dot(lower.astype(BF16), jnp.broadcast_to(tiles, (GROUPS, 128)).astype(BF16))[:, 0:1]
    for g in range(GROUPS):
        first_ref[g] = jnp.sum(start[g : g + 1]).astype(I32)
    first_ref[GROUPS] = jnp.sum(tiles).astype(I32)
    used = first_ref[GROUPS]

    def name_group(g, carry):
        def name_tile(t, inner):
            group_ref[t] = g
            return inner

        return lax.fori_loop(first_ref[g], first_ref[g + 1], name_tile, carry)

    lax.fori_loop(0, GROUPS, name_group, 0)
    for n in range(PAIR - 1):
        group_ref[used + n] = 0

    sorted_ref[...] = jnp.zeros_like(sorted_ref)

    def sort(n, first, rows):
        lanes = pl.ds(pl.multiple_of(n * C_LANES, C_LANES), C_LANES)
        group = data_ref[4:5, lanes].astype(I32)
        here = iota((GROUPS, C_LANES), 0) == group
        base = jnp.sum(jnp.where(here, start, 0.0), axis=0, keepdims=True)
        slot = base.astype(I32) * TILE + data_ref[5:6, lanes].astype(I32)
        where_row = onehot(first, rows, jnp.where(group < GROUPS, slot >> 8, -1))
        where_col = onehot(0, TILE, slot & 255)
        at = iota((1, C_LANES), 1)
        pair = n * (SOURCES // 2) + ((at >> 7) & (SOURCES // 2 - 1))
        third = at >= SOURCES * 128
        odd = jnp.where(third, (at >> 6) & 1, jnp.where(at >= SOURCES * 64, 1, 0))
        back = flat_slot(2 * pair + odd, jnp.where(third, 128 + (at & 63), at & 127))
        lhs = [both(where_row, *parts(data_ref[k : k + 1, lanes])) for k in range(3)]
        lhs.append(both(where_row, ((back >> 8) + 1) * 64, data_ref[3:4, lanes]))
        wide = jnp.concatenate([where_col, where_col], axis=1)
        got = lane_dot(jnp.concatenate(lhs, axis=0), wide)
        last = lane_dot(spread(where_row, back & 255), where_col)
        for k in range(4):
            sorted_ref[k, first : first + rows, :] += got[k * rows : k * rows + rows]
        sorted_ref[4, first : first + rows, :] += last

    def usual(n, carry):
        sort(n, 0, USUAL)
        return carry

    lax.fori_loop(0, STEPS, usual, 0)

    @pl.when(used > USUAL)
    def _():
        def more(n, carry):
            sort(n, USUAL, MOST - USUAL)
            return carry

        lax.fori_loop(0, STEPS, more, 0)

    val_ref[...] = jnp.zeros_like(val_ref)
    load.wait()
    row8 = iota((8, TILE), 0)
    scales = jnp.zeros((8, TILE), F32)
    for i in range(8):
        value = 1.0
        for n in range(8):
            if n != i:
                value = value / (nodes[i] - nodes[n])
        scales = jnp.where(row8 == i, float(value), scales)

    def one_tile(t):
        rows = pl.ds(pl.multiple_of(group_ref[t] * GROUP, GROUP), GROUP)
        table = jnp.concatenate(
            [file_ref[rows, f * 512 : f * 512 + 512] for f in range(FIELDS)], axis=0
        )
        table = jnp.concatenate([table, table], axis=1)
        b0, b1, b2 = [basis_rows(from_grid(sorted_ref[k, pl.ds(t, 1), :]), nodes, scales) for k in range(3)]
        element = sorted_ref[3, pl.ds(t, 1), :].astype(I32) & 63
        planes = jnp.concatenate([b1[j : j + 1] * b2 for j in range(8)], axis=0)
        tops, lows = [], []
        for i in range(8):
            tensor = b0[i : i + 1] * planes
            top = tensor.astype(BF16)
            tops.append(top)
            lows.append((tensor - top.astype(F32)).astype(BF16))
        result = dot(table, jnp.concatenate(tops + lows, axis=0))
        mask = iota((GROUP, TILE), 0) == element
        return [
            jnp.sum(
                jnp.where(mask, result[f * GROUP : f * GROUP + GROUP], 0.0), axis=0, keepdims=True
            )
            for f in range(FIELDS)
        ]

    def on_tiles(n, carry):
        values = [one_tile(n * PAIR + q) for q in range(PAIR)]
        for q in range(PAIR):
            for f in range(FIELDS):
                val_ref[f, pl.ds(n * PAIR + q, 1), :] = values[q][f]
        return carry

    lax.fori_loop(0, (used + PAIR - 1) // PAIR, on_tiles, 0)

    acc_ref[...] = jnp.zeros_like(acc_ref)

    def back(n, carry):
        def row(ref, k):
            lines = [ref[k, pl.ds(n * MANY + q, 1), :] for q in range(MANY)]
            return jnp.concatenate(lines, axis=1)

        where_row = onehot(0, ROWS, (row(sorted_ref, 3).astype(I32) >> 6) - 1)
        where_col = onehot(0, 256, row(sorted_ref, 4))
        wide = jnp.concatenate([where_col, where_col], axis=1)
        lhs = [both(where_row, *parts(row(val_ref, f))) for f in range(FIELDS)]
        acc_ref[...] += lane_dot(jnp.concatenate(lhs, axis=0), wide)
        return carry

    lax.fori_loop(0, (used + MANY - 1) // MANY, back, 0)
    evens, odds, middle = [], [], []
    for f in range(FIELDS):
        block = acc_ref[f * ROWS : f * ROWS + ROWS, :]
        flat_ref[pl.ds(0, ROWS, 2), :] = block[:, 0:128]
        flat_ref[pl.ds(1, ROWS, 2), :] = block[:, 128:256]
        evens.append(flat_ref[pl.ds(0, 64, 3), :])
        odds.append(flat_ref[pl.ds(2, 64, 3), :])
        middle.append(flat_ref[pl.ds(1, 64, 3), :])
    low = iota((64, 128), 1) < HALF

    def exponent(firsts, own):
        most = jnp.zeros((64, 128), F32)
        for first, mid in zip(firsts, middle):
            most = jnp.maximum(most, jnp.abs(first))
            most = jnp.maximum(most, jnp.where(own, jnp.abs(mid), 0.0))
        most = jnp.max(most, axis=1, keepdims=True)
        power = jnp.ceil(jnp.log2(jnp.maximum(most, 1e-30)))
        return jnp.broadcast_to(power, (64, 128))

    def coded(value, factor):
        return jnp.floor(value * factor + 0.5).astype(I32)

    def word(a, b):
        return (a & 0xFFFF) | (b << 16)

    powers = [exponent(evens, low), exponent(odds, jnp.logical_not(low))]
    factors = [LEVELS * jnp.exp2(-power) for power in powers]
    last = [coded(mid, jnp.where(low, factors[0], factors[1])) for mid in middle]
    for odd, firsts in enumerate((evens, odds)):
        halves = right_halves if odd else left_halves
        first = [coded(value, factors[odd]) for value in firsts]
        power = powers[odd].astype(I32)
        out_ref[:, 4 * odd, :] = word(first[0], first[1])
        out_ref[:, 4 * odd + 1, :] = word(first[2], first[3])
        out_ref[:, 4 * odd + 2, :] = word(first[4], halves(last[0], last[1]))
        tail = pltpu.roll(last[3], HALF, 1) if odd else last[3]
        out_ref[:, 4 * odd + 3, :] = word(halves(last[2], last[4]), jnp.where(low, tail, power))


def evaluate(recv, span, file_fields):
    return pl.pallas_call(
        evaluate_kernel,
        out_shape=jax.ShapeDtypeStruct((DEVICES // 2, 8, 128), I32),
        in_specs=[
            pl.BlockSpec(memory_space=pltpu.VMEM),
            pl.BlockSpec(memory_space=pltpu.VMEM),
            pl.BlockSpec(memory_space=pl.ANY),
        ],
        out_specs=pl.BlockSpec(memory_space=pltpu.VMEM),
        scratch_shapes=[
            pltpu.VMEM((DEVICES * SPAN, WIDTH), BF16),
            pltpu.VMEM((8, SLOTS), F32),
            pltpu.VMEM((5, MOST, TILE), F32),
            pltpu.VMEM((FIELDS, MOST, TILE), F32),
            pltpu.VMEM((FIELDS * ROWS, 256), F32),
            pltpu.VMEM((2 * ROWS, 128), F32),
            pltpu.SMEM((GROUPS + 1,), I32),
            pltpu.SMEM((MOST + PAIR,), I32),
            pltpu.SemaphoreType.DMA(()),
        ],
        compiler_params=pltpu.CompilerParams(vmem_limit_bytes=50 * 1024 * 1024),
        cost_estimate=pl.CostEstimate(
            flops=60_000_000_000, bytes_accessed=6_000_000, transcendentals=0
        ),
        name="evaluate",
    )(recv, span, file_fields)


E_LANES = 2048
PIECES = 4


def collect_kernel(
    back_ref, slot_ref, moved_hbm, out_ref, owned_hbm, table_ref, flat_ref, held_ref, sems
):
    rows = DEVICES * SPAN // PIECES
    pieces = [pl.ds(n * rows, rows) for n in range(PIECES)]
    loads = [
        pltpu.make_async_copy(moved_hbm.at[p], held_ref.at[p], sems.at[n])
        for n, p in enumerate(pieces)
    ]
    stores = [
        pltpu.make_async_copy(held_ref.at[p], owned_hbm.at[p], sems.at[PIECES + n])
        for n, p in enumerate(pieces)
    ]
    for copy in loads:
        copy.start()
    firsts, lasts = [], []
    for odd in range(2):
        words = [back_ref[:, 4 * odd + r, :] for r in range(4)]
        tail = high_half(words[3])
        factor = jnp.exp2(right_halves(tail, tail).astype(F32)) * (1.0 / LEVELS)
        firsts.append(
            [
                half(words[r]).astype(F32) * factor
                for r, half in (
                    (0, low_half), (0, high_half), (1, low_half), (1, high_half), (2, low_half)
                )
            ]
        )
        lasts.append(
            [
                value.astype(F32) * factor
                for value in (high_half(words[2]), low_half(words[3]), tail)
            ]
        )
    for f in range(FIELDS):
        flat_ref[pl.ds(0, 64, 3), :] = firsts[0][f]
        flat_ref[pl.ds(2, 64, 3), :] = firsts[1][f]
        k, halves = ((0, left_halves), (0, right_halves), (1, left_halves), (2, left_halves), (1, right_halves))[f]
        flat_ref[pl.ds(1, 64, 3), :] = halves(lasts[0][k], lasts[1][k])
        for half in range(2):
            high, rest = parts(flat_ref[pl.ds(half, ROWS, 2), :])
            here = slice(f * ROWS, f * ROWS + ROWS)
            table_ref[here, 128 * half : 128 * half + 128] = high.astype(BF16)
            table_ref[here, 256 + 128 * half : 384 + 128 * half] = rest.astype(BF16)

    def step(n, carry):
        lanes = pl.ds(pl.multiple_of(n * E_LANES, E_LANES), E_LANES)
        slot = slot_ref[:, lanes]
        mask = iota((ROWS, E_LANES), 0) == (slot >> 8)
        where_col = onehot(0, 256, slot & 255)
        got = dot(table_ref[...], jnp.concatenate([where_col, where_col], axis=0))
        for f in range(FIELDS):
            out_ref[f : f + 1, lanes] = jnp.sum(
                jnp.where(mask, got[f * ROWS : f * ROWS + ROWS], 0.0), axis=0, keepdims=True
            )
        return carry

    steps = POINTS // E_LANES
    lax.fori_loop(0, steps // 2, step, 0, unroll=True)
    for load, store in zip(loads, stores):
        load.wait()
        store.start()
    lax.fori_loop(steps // 2, steps, step, 0, unroll=True)
    for store in stores:
        store.wait()


def collect(back, slot, moved):
    return pl.pallas_call(
        collect_kernel,
        out_shape=(
            jax.ShapeDtypeStruct((FIELDS, POINTS), F32),
            jax.ShapeDtypeStruct(moved.shape, moved.dtype),
        ),
        in_specs=[
            pl.BlockSpec(memory_space=pltpu.VMEM),
            pl.BlockSpec(memory_space=pltpu.VMEM),
            pl.BlockSpec(memory_space=pl.ANY),
        ],
        out_specs=(pl.BlockSpec(memory_space=pltpu.VMEM), pl.BlockSpec(memory_space=pl.ANY)),
        scratch_shapes=[
            pltpu.VMEM((FIELDS * ROWS, 512), BF16),
            pltpu.VMEM((2 * ROWS, 128), F32),
            pltpu.VMEM((DEVICES * SPAN, WIDTH), BF16),
            pltpu.SemaphoreType.DMA((2 * PIECES,)),
        ],
        compiler_params=pltpu.CompilerParams(vmem_limit_bytes=56 * 1024 * 1024),
        name="collect",
    )(back, slot, moved)


def exchange(x):
    return lax.all_to_all(x, AXES, split_axis=0, concat_axis=0, tiled=True)


def shards(file_fields, span_map, point_dest, point_local, point_coords):
    columns = jnp.arange(DEVICES, dtype=I32)
    inverse = jnp.zeros((DEVICES,), I32).at[span_map[0]].set(columns)
    pieces = file_fields.reshape(DEVICES, SPAN, WIDTH)[inverse]
    sent, slot = bucket(
        point_dest.reshape(1, POINTS), point_local.reshape(1, POINTS), point_coords
    )
    recv = exchange(sent.reshape(DEVICES, 4, 128)).reshape(DEVICES // 2, 8, 128)
    pieces, recv = lax.optimization_barrier((pieces, recv))
    moved = exchange(pieces).reshape(DEVICES * SPAN, WIDTH)
    values = evaluate(recv, span_map, file_fields)
    values, moved = lax.optimization_barrier((values, moved))
    back = exchange(values.reshape(DEVICES, 4, 128)).reshape(DEVICES // 2, 8, 128)
    return collect(back, slot, moved)


def solution(mesh):
    return jax.shard_map(
        shards,
        mesh=mesh,
        in_specs=(
            P(AXES, None),
            P(AXES, None),
            P(AXES, None),
            P(AXES),
            P(None, AXES),
        ),
        out_specs=(P(None, AXES), P(AXES, None)),
        check_vma=False,
    )
```

```python
import jax
import jax.numpy as jnp
import numpy as np
from jax import lax
from jax.experimental import pallas as pl
from jax.experimental.pallas import tpu as pltpu
from jax.sharding import PartitionSpec as P

NODES = 8
FIELDS = 5
SPAN = 8
DEVICES = 128
POINTS = 16384
CAP = 192
HALF = 64
WIDTH = FIELDS * NODES**3
SLOTS = DEVICES * CAP
GROUP = 64
GROUPS = 16
TILE = 256
ROWS = SLOTS // 256
MOST = SLOTS // TILE + GROUPS
AXES = ("owner", "sub")
F32 = jnp.float32
BF16 = jnp.bfloat16
I32 = jnp.int32


def gll_nodes(count):
    order = count - 1
    points = np.cos(np.pi * np.arange(count) / order)
    for sweep in range(100):
        oldest = np.ones(count)
        recent = points * 1.0
        for degree in range(2, order + 1):
            newest = ((2 * degree - 1) * points * recent - (degree - 1) * oldest) / degree
            oldest = recent
            recent = newest
        points = points - (points * recent - oldest) / (count * recent)
    return points[::-1]


def iota(shape, dim):
    return lax.broadcasted_iota(I32, shape, dim)


def lane_dot(a, b):
    return lax.dot_general(a, b, (((1,), (1,)), ((), ())), preferred_element_type=F32)


def dot(a, b):
    return jnp.dot(a, b, preferred_element_type=F32)


def parts(x):
    high = x.astype(BF16).astype(F32)
    return high, x - high


def earlier(rows, cols):
    return jnp.where(iota((rows, cols), 0) < iota((rows, cols), 1), 1.0, 0.0).astype(BF16)


def packed(value):
    return jnp.broadcast_to(value.astype(F32), (16, value.shape[1])).astype(BF16)


def onehot(first, rows, value):
    value = packed(value)
    base = iota(value.shape, 0)
    one, zero = jnp.asarray(1.0, BF16), jnp.asarray(0.0, BF16)
    out = []
    for r in range(rows // 16):
        out.append(jnp.where((base + (first + 16 * r)).astype(F32).astype(BF16) == value, one, zero))
    return jnp.concatenate(out, axis=0)


def spread(ones, value):
    value = packed(value)
    return jnp.concatenate(
        [ones[16 * r : 16 * r + 16] * value for r in range(ones.shape[0] // 16)], axis=0
    )


def both(ones, high, low):
    return jnp.concatenate([spread(ones, high), spread(ones, low)], axis=1)


def ranks(mask, before, base):
    ones = jnp.where(mask, 1.0, 0.0)
    narrow = ones.astype(BF16)
    counts = []
    rows, blocks = mask.shape[0], mask.shape[1] // 256
    stacked = [narrow[:, 256 * j : 256 * j + 256] for j in range(blocks)]
    stacked = dot(jnp.concatenate(stacked, axis=0), before)
    for j in range(blocks):
        inside = stacked[rows * j : rows * j + rows]
        counts.append(inside + base)
        base = base + inside[:, 255:256] + ones[:, 256 * j + 255 : 256 * j + 256]
    count = jnp.concatenate(counts, axis=1)
    return jnp.sum(jnp.where(mask, count, 0.0), axis=0, keepdims=True), base


def flat_slot(block, place):
    odd = (block & 1) == 1
    late = place >= 128
    return block * CAP + jnp.where(odd, jnp.where(late, place - 128, place + 64), place)


def to_grid(x):
    return ((x + 1.0) * 32767.5 + 0.5).astype(I32).astype(F32)


def from_grid(x):
    return x * (1.0 / 32767.5) - 1.0


def low_half(word):
    return (word << 16) >> 16


def high_half(word):
    return word >> 16


def left_halves(a, b):
    return jnp.where(iota(a.shape, 1) < HALF, a, pltpu.roll(b, HALF, 1))


def right_halves(a, b):
    return jnp.where(iota(a.shape, 1) < HALF, pltpu.roll(a, HALF, 1), b)


A_LANES = 4096


def bucket_kernel(
    dest_hbm, local_hbm, coords_hbm, out_ref, slot_ref, dest_ref, local_ref, coords_ref, acc_ref, flat_ref, sems
):
    early, late = pl.ds(0, A_LANES), pl.ds(A_LANES, POINTS - A_LANES)
    copies = [
        pltpu.make_async_copy(src, dst, sems.at[n])
        for n, (src, dst) in enumerate(
            [
                (local_hbm.at[:, early], local_ref.at[:, early]),
                (local_hbm.at[:, late], local_ref.at[:, late]),
                (dest_hbm, dest_ref),
                (coords_hbm, coords_ref),
            ]
        )
    ]
    for copy in copies:
        copy.start()
    acc_ref[...] = jnp.zeros_like(acc_ref)
    before = earlier(256, 256)
    steps = POINTS // A_LANES

    def at(n):
        return pl.ds(pl.multiple_of(n * A_LANES, A_LANES), A_LANES)

    def place(n, base):
        holder = local_ref[:, at(n)] >> 3
        rank, base = ranks(iota((DEVICES, A_LANES), 0) == holder, before, base)
        slot_ref[:, at(n)] = flat_slot(holder, rank.astype(I32))
        return base

    def scatter(n):
        slot = slot_ref[:, at(n)]
        where_row = onehot(0, ROWS, slot >> 8)
        where_col = onehot(0, 256, slot & 255)
        local = local_ref[:, at(n)]
        rows = []
        for k in range(3):
            clear = (1 - ((local >> k) & 1)) * 65536
            grid = to_grid(coords_ref[k : k + 1, at(n)]) - clear.astype(F32)
            rows += [spread(where_row, part) for part in parts(grid)]
        rows.append(spread(where_row, dest_ref[:, at(n)] + 1))
        return lane_dot(jnp.concatenate(rows, axis=0), where_col)

    copies[0].wait()
    base = place(0, jnp.zeros((DEVICES, 1), F32))
    for copy in copies[1:]:
        copy.wait()

    def step(n, base):
        got = scatter(n)
        base = place(n + 1, base)
        acc_ref[...] += got
        return base

    lax.fori_loop(0, steps - 1, step, base)
    acc_ref[...] += scatter(steps - 1)
    fields = [acc_ref[k * ROWS : k * ROWS + ROWS, :].astype(I32) for k in range(7)]
    fields = [fields[0] + fields[1], fields[2] + fields[3], fields[4] + fields[5], fields[6]]
    number = fields[3] * 8
    for k in range(3):
        signed = fields[k] + 65536
        number = number + ((signed >> 16) << k)
        fields[k] = signed & 0xFFFF
    fields[3] = jnp.where(fields[3] > 0, number, 0)
    middle = []
    for k in range(2):
        low, high = fields[2 * k], fields[2 * k + 1]
        block = low + (high << 16)
        flat_ref[pl.ds(0, ROWS, 2), :] = block[:, 0:128]
        flat_ref[pl.ds(1, ROWS, 2), :] = block[:, 128:256]
        out_ref[:, k, :] = flat_ref[pl.ds(0, 64, 3), :]
        out_ref[:, 4 + k, :] = flat_ref[pl.ds(2, 64, 3), :]
        middle.append(flat_ref[pl.ds(1, 64, 3), :])
    out_ref[:, 2, :] = left_halves(*middle)
    out_ref[:, 6, :] = right_halves(*middle)
    out_ref[:, 3, :] = jnp.zeros((64, 128), I32)
    out_ref[:, 7, :] = jnp.zeros((64, 128), I32)


def bucket(dest, local, coords):
    return pl.pallas_call(
        bucket_kernel,
        out_shape=(
            jax.ShapeDtypeStruct((DEVICES // 2, 8, 128), I32),
            jax.ShapeDtypeStruct((1, POINTS), I32),
        ),
        in_specs=[pl.BlockSpec(memory_space=pl.ANY)] * 3,
        out_specs=(pl.BlockSpec(memory_space=pltpu.VMEM),) * 2,
        scratch_shapes=[
            pltpu.VMEM((1, POINTS), I32),
            pltpu.VMEM((1, POINTS), I32),
            pltpu.VMEM((3, POINTS), F32),
            pltpu.VMEM((7 * ROWS, 256), F32),
            pltpu.VMEM((2 * ROWS, 128), I32),
            pltpu.SemaphoreType.DMA((4,)),
        ],
        compiler_params=pltpu.CompilerParams(vmem_limit_bytes=56 * 1024 * 1024),
        name="bucket",
    )(dest, local, coords)


SOURCES = 32
C_LANES = SOURCES * CAP
STEPS = DEVICES // SOURCES
USUAL = 96
LEVELS = 32600.0
PAIR = 8
MANY = 16


def basis_rows(x, nodes, scale):
    row = iota((8, x.shape[1]), 0)
    out = None
    for n in range(8):
        term = jnp.where(row == n, scale, x - float(nodes[n]))
        out = term if out is None else out * term
    return out


def evaluate_kernel(
    recv_ref, span_ref, file_hbm, out_ref, file_ref, data_ref, sorted_ref, val_ref, acc_ref, flat_ref, first_ref, group_ref, sem
):
    load = pltpu.make_async_copy(file_hbm, file_ref, sem)
    load.start()
    nodes = gll_nodes(NODES)
    before = earlier(256, 256)
    permutation = jnp.where(iota((128, 128), 0) == span_ref[...], 1.0, 0.0).astype(BF16)
    inverse = lane_dot(iota((16, 128), 1).astype(F32).astype(BF16), permutation).astype(BF16)

    def count(n, base):
        blocks = [recv_ref[n * (SOURCES // 2) + s] for s in range(SOURCES // 2)]
        turned = [pltpu.roll(block, HALF, 1) for block in blocks]
        whole = jnp.concatenate(blocks, axis=1)
        swapped = jnp.concatenate(turned, axis=1)
        early = (iota((1, SOURCES * 64), 1) & 127) < HALF
        words = [
            jnp.concatenate(
                [whole[0:1], whole[4:5], jnp.where(early, whole[2:3], swapped[6:7])], axis=1
            ),
            jnp.concatenate(
                [whole[1:2], whole[5:6], jnp.where(early, swapped[2:3], whole[6:7])], axis=1
            ),
        ]
        number = high_half(words[1])
        span = dot(inverse, onehot(0, 128, (number >> 3) - 1))[0:1].astype(I32)
        group = jnp.where(number > 0, span >> 3, GROUPS)
        element = (span & 7) * 8 + (number & 7)
        rank, base = ranks(iota((GROUPS, C_LANES), 0) == group, before, base)
        lanes = pl.ds(pl.multiple_of(n * C_LANES, C_LANES), C_LANES)
        data_ref[0:1, lanes] = (words[0] & 0xFFFF).astype(F32)
        data_ref[1:2, lanes] = (high_half(words[0]) & 0xFFFF).astype(F32)
        data_ref[2:3, lanes] = (words[1] & 0xFFFF).astype(F32)
        data_ref[3:4, lanes] = element.astype(F32)
        data_ref[4:5, lanes] = group.astype(F32)
        data_ref[5:6, lanes] = rank
        return base

    total = lax.fori_loop(0, STEPS, count, jnp.zeros((GROUPS, 1), F32))
    tiles = ((total.astype(I32) + (TILE - 1)) >> 8).astype(F32)
    lower = jnp.where(iota((GROUPS, GROUPS), 1) < iota((GROUPS, GROUPS), 0), 1.0, 0.0)
    start = dot(lower.astype(BF16), jnp.broadcast_to(tiles, (GROUPS, 128)).astype(BF16))[:, 0:1]
    for g in range(GROUPS):
        first_ref[g] = jnp.sum(start[g : g + 1]).astype(I32)
    first_ref[GROUPS] = jnp.sum(tiles).astype(I32)
    used = first_ref[GROUPS]

    def name_group(g, carry):
        def name_tile(t, inner):
            group_ref[t] = g
            return inner

        return lax.fori_loop(first_ref[g], first_ref[g + 1], name_tile, carry)

    lax.fori_loop(0, GROUPS, name_group, 0)
    for n in range(PAIR - 1):
        group_ref[used + n] = 0

    sorted_ref[...] = jnp.zeros_like(sorted_ref)

    def sort(n, first, rows):
        lanes = pl.ds(pl.multiple_of(n * C_LANES, C_LANES), C_LANES)
        group = data_ref[4:5, lanes].astype(I32)
        here = iota((GROUPS, C_LANES), 0) == group
        base = jnp.sum(jnp.where(here, start, 0.0), axis=0, keepdims=True)
        slot = base.astype(I32) * TILE + data_ref[5:6, lanes].astype(I32)
        where_row = onehot(first, rows, jnp.where(group < GROUPS, slot >> 8, -1))
        where_col = onehot(0, TILE, slot & 255)
        at = iota((1, C_LANES), 1)
        pair = n * (SOURCES // 2) + ((at >> 7) & (SOURCES // 2 - 1))
        third = at >= SOURCES * 128
        odd = jnp.where(third, (at >> 6) & 1, jnp.where(at >= SOURCES * 64, 1, 0))
        back = flat_slot(2 * pair + odd, jnp.where(third, 128 + (at & 63), at & 127))
        lhs = [both(where_row, *parts(data_ref[k : k + 1, lanes])) for k in range(3)]
        lhs.append(both(where_row, ((back >> 8) + 1) * 64, data_ref[3:4, lanes]))
        wide = jnp.concatenate([where_col, where_col], axis=1)
        got = lane_dot(jnp.concatenate(lhs, axis=0), wide)
        last = lane_dot(spread(where_row, back & 255), where_col)
        for k in range(4):
            sorted_ref[k, first : first + rows, :] += got[k * rows : k * rows + rows]
        sorted_ref[4, first : first + rows, :] += last

    def usual(n, carry):
        sort(n, 0, USUAL)
        return carry

    lax.fori_loop(0, STEPS, usual, 0)

    @pl.when(used > USUAL)
    def _():
        def more(n, carry):
            sort(n, USUAL, MOST - USUAL)
            return carry

        lax.fori_loop(0, STEPS, more, 0)

    val_ref[...] = jnp.zeros_like(val_ref)
    load.wait()
    row8 = iota((8, TILE), 0)
    scales = jnp.zeros((8, TILE), F32)
    for i in range(8):
        value = 1.0
        for n in range(8):
            if n != i:
                value = value / (nodes[i] - nodes[n])
        scales = jnp.where(row8 == i, float(value), scales)

    def one_tile(t):
        rows = pl.ds(pl.multiple_of(group_ref[t] * GROUP, GROUP), GROUP)
        table = jnp.concatenate(
            [file_ref[rows, f * 512 : f * 512 + 512] for f in range(FIELDS)], axis=0
        )
        table = jnp.concatenate([table, table], axis=1)
        b0, b1, b2 = [basis_rows(from_grid(sorted_ref[k, pl.ds(t, 1), :]), nodes, scales) for k in range(3)]
        element = sorted_ref[3, pl.ds(t, 1), :].astype(I32) & 63
        planes = jnp.concatenate([b1[j : j + 1] * b2 for j in range(8)], axis=0)
        tops, lows = [], []
        for i in range(8):
            tensor = b0[i : i + 1] * planes
            top = tensor.astype(BF16)
            tops.append(top)
            lows.append((tensor - top.astype(F32)).astype(BF16))
        result = dot(table, jnp.concatenate(tops + lows, axis=0))
        mask = iota((GROUP, TILE), 0) == element
        return [
            jnp.sum(
                jnp.where(mask, result[f * GROUP : f * GROUP + GROUP], 0.0), axis=0, keepdims=True
            )
            for f in range(FIELDS)
        ]

    def on_tiles(n, carry):
        values = [one_tile(n * PAIR + q) for q in range(PAIR)]
        for q in range(PAIR):
            for f in range(FIELDS):
                val_ref[f, pl.ds(n * PAIR + q, 1), :] = values[q][f]
        return carry

    lax.fori_loop(0, (used + PAIR - 1) // PAIR, on_tiles, 0)

    acc_ref[...] = jnp.zeros_like(acc_ref)

    def back(n, carry):
        def row(ref, k):
            lines = [ref[k, pl.ds(n * MANY + q, 1), :] for q in range(MANY)]
            return jnp.concatenate(lines, axis=1)

        where_row = onehot(0, ROWS, (row(sorted_ref, 3).astype(I32) >> 6) - 1)
        where_col = onehot(0, 256, row(sorted_ref, 4))
        wide = jnp.concatenate([where_col, where_col], axis=1)
        lhs = [both(where_row, *parts(row(val_ref, f))) for f in range(FIELDS)]
        acc_ref[...] += lane_dot(jnp.concatenate(lhs, axis=0), wide)
        return carry

    lax.fori_loop(0, (used + MANY - 1) // MANY, back, 0)
    evens, odds, middle = [], [], []
    for f in range(FIELDS):
        block = acc_ref[f * ROWS : f * ROWS + ROWS, :]
        flat_ref[pl.ds(0, ROWS, 2), :] = block[:, 0:128]
        flat_ref[pl.ds(1, ROWS, 2), :] = block[:, 128:256]
        evens.append(flat_ref[pl.ds(0, 64, 3), :])
        odds.append(flat_ref[pl.ds(2, 64, 3), :])
        middle.append(flat_ref[pl.ds(1, 64, 3), :])
    low = iota((64, 128), 1) < HALF

    def exponent(firsts, own):
        most = jnp.zeros((64, 128), F32)
        for first, mid in zip(firsts, middle):
            most = jnp.maximum(most, jnp.abs(first))
            most = jnp.maximum(most, jnp.where(own, jnp.abs(mid), 0.0))
        most = jnp.max(most, axis=1, keepdims=True)
        power = jnp.ceil(jnp.log2(jnp.maximum(most, 1e-30)))
        return jnp.broadcast_to(power, (64, 128))

    def coded(value, factor):
        return jnp.floor(value * factor + 0.5).astype(I32)

    def word(a, b):
        return (a & 0xFFFF) | (b << 16)

    powers = [exponent(evens, low), exponent(odds, jnp.logical_not(low))]
    factors = [LEVELS * jnp.exp2(-power) for power in powers]
    last = [coded(mid, jnp.where(low, factors[0], factors[1])) for mid in middle]
    for odd, firsts in enumerate((evens, odds)):
        halves = right_halves if odd else left_halves
        first = [coded(value, factors[odd]) for value in firsts]
        power = powers[odd].astype(I32)
        out_ref[:, 4 * odd, :] = word(first[0], first[1])
        out_ref[:, 4 * odd + 1, :] = word(first[2], first[3])
        out_ref[:, 4 * odd + 2, :] = word(first[4], halves(last[0], last[1]))
        tail = pltpu.roll(last[3], HALF, 1) if odd else last[3]
        out_ref[:, 4 * odd + 3, :] = word(halves(last[2], last[4]), jnp.where(low, tail, power))


def evaluate(recv, span, file_fields):
    return pl.pallas_call(
        evaluate_kernel,
        out_shape=jax.ShapeDtypeStruct((DEVICES // 2, 8, 128), I32),
        in_specs=[
            pl.BlockSpec(memory_space=pltpu.VMEM),
            pl.BlockSpec(memory_space=pltpu.VMEM),
            pl.BlockSpec(memory_space=pl.ANY),
        ],
        out_specs=pl.BlockSpec(memory_space=pltpu.VMEM),
        scratch_shapes=[
            pltpu.VMEM((DEVICES * SPAN, WIDTH), BF16),
            pltpu.VMEM((8, SLOTS), F32),
            pltpu.VMEM((5, MOST, TILE), F32),
            pltpu.VMEM((FIELDS, MOST, TILE), F32),
            pltpu.VMEM((FIELDS * ROWS, 256), F32),
            pltpu.VMEM((2 * ROWS, 128), F32),
            pltpu.SMEM((GROUPS + 1,), I32),
            pltpu.SMEM((MOST + PAIR,), I32),
            pltpu.SemaphoreType.DMA(()),
        ],
        compiler_params=pltpu.CompilerParams(vmem_limit_bytes=50 * 1024 * 1024),
        cost_estimate=pl.CostEstimate(
            flops=60_000_000_000, bytes_accessed=6_000_000, transcendentals=0
        ),
        name="evaluate",
    )(recv, span, file_fields)


E_LANES = 2048
PIECES = 4


def collect_kernel(
    back_ref, slot_ref, moved_hbm, out_ref, owned_hbm, table_ref, flat_ref, held_ref, sems
):
    rows = DEVICES * SPAN // PIECES
    pieces = [pl.ds(n * rows, rows) for n in range(PIECES)]
    loads = [
        pltpu.make_async_copy(moved_hbm.at[p], held_ref.at[p], sems.at[n])
        for n, p in enumerate(pieces)
    ]
    stores = [
        pltpu.make_async_copy(held_ref.at[p], owned_hbm.at[p], sems.at[PIECES + n])
        for n, p in enumerate(pieces)
    ]
    for copy in loads:
        copy.start()
    firsts, lasts = [], []
    for odd in range(2):
        words = [back_ref[:, 4 * odd + r, :] for r in range(4)]
        tail = high_half(words[3])
        factor = jnp.exp2(right_halves(tail, tail).astype(F32)) * (1.0 / LEVELS)
        firsts.append(
            [
                half(words[r]).astype(F32) * factor
                for r, half in (
                    (0, low_half), (0, high_half), (1, low_half), (1, high_half), (2, low_half)
                )
            ]
        )
        lasts.append(
            [
                value.astype(F32) * factor
                for value in (high_half(words[2]), low_half(words[3]), tail)
            ]
        )
    for f in range(FIELDS):
        flat_ref[pl.ds(0, 64, 3), :] = firsts[0][f]
        flat_ref[pl.ds(2, 64, 3), :] = firsts[1][f]
        k, halves = ((0, left_halves), (0, right_halves), (1, left_halves), (2, left_halves), (1, right_halves))[f]
        flat_ref[pl.ds(1, 64, 3), :] = halves(lasts[0][k], lasts[1][k])
        for half in range(2):
            high, rest = parts(flat_ref[pl.ds(half, ROWS, 2), :])
            here = slice(f * ROWS, f * ROWS + ROWS)
            table_ref[here, 128 * half : 128 * half + 128] = high.astype(BF16)
            table_ref[here, 256 + 128 * half : 384 + 128 * half] = rest.astype(BF16)

    def step(n, carry):
        lanes = pl.ds(pl.multiple_of(n * E_LANES, E_LANES), E_LANES)
        slot = slot_ref[:, lanes]
        mask = iota((ROWS, E_LANES), 0) == (slot >> 8)
        where_col = onehot(0, 256, slot & 255)
        got = dot(table_ref[...], jnp.concatenate([where_col, where_col], axis=0))
        for f in range(FIELDS):
            out_ref[f : f + 1, lanes] = jnp.sum(
                jnp.where(mask, got[f * ROWS : f * ROWS + ROWS], 0.0), axis=0, keepdims=True
            )
        return carry

    steps = POINTS // E_LANES
    lax.fori_loop(0, steps // 2, step, 0, unroll=True)
    for load, store in zip(loads, stores):
        load.wait()
        store.start()
    lax.fori_loop(steps // 2, steps, step, 0, unroll=True)
    for store in stores:
        store.wait()


def collect(back, slot, moved):
    return pl.pallas_call(
        collect_kernel,
        out_shape=(
            jax.ShapeDtypeStruct((FIELDS, POINTS), F32),
            jax.ShapeDtypeStruct(moved.shape, moved.dtype),
        ),
        in_specs=[
            pl.BlockSpec(memory_space=pltpu.VMEM),
            pl.BlockSpec(memory_space=pltpu.VMEM),
            pl.BlockSpec(memory_space=pl.ANY),
        ],
        out_specs=(pl.BlockSpec(memory_space=pltpu.VMEM), pl.BlockSpec(memory_space=pl.ANY)),
        scratch_shapes=[
            pltpu.VMEM((FIELDS * ROWS, 512), BF16),
            pltpu.VMEM((2 * ROWS, 128), F32),
            pltpu.VMEM((DEVICES * SPAN, WIDTH), BF16),
            pltpu.SemaphoreType.DMA((2 * PIECES,)),
        ],
        compiler_params=pltpu.CompilerParams(vmem_limit_bytes=56 * 1024 * 1024),
        name="collect",
    )(back, slot, moved)


def exchange(x):
    return lax.all_to_all(x, AXES, split_axis=0, concat_axis=0, tiled=True)


def shards(file_fields, span_map, point_dest, point_local, point_coords):
    columns = jnp.arange(DEVICES, dtype=I32)
    inverse = jnp.zeros((DEVICES,), I32).at[span_map[0]].set(columns)
    pieces = file_fields.reshape(DEVICES, SPAN, WIDTH)[inverse]
    sent, slot = bucket(
        point_dest.reshape(1, POINTS), point_local.reshape(1, POINTS), point_coords
    )
    recv = exchange(sent.reshape(DEVICES, 4, 128)).reshape(DEVICES // 2, 8, 128)
    pieces, recv = lax.optimization_barrier((pieces, recv))
    moved = exchange(pieces).reshape(DEVICES * SPAN, WIDTH)
    values = evaluate(recv, span_map, file_fields)
    values, moved = lax.optimization_barrier((values, moved))
    back = exchange(values.reshape(DEVICES, 4, 128)).reshape(DEVICES // 2, 8, 128)
    return collect(back, slot, moved)


def solution(mesh):
    return jax.shard_map(
        shards,
        mesh=mesh,
        in_specs=(
            P(AXES, None),
            P(AXES, None),
            P(AXES, None),
            P(AXES),
            P(None, AXES),
        ),
        out_specs=(P(None, AXES), P(AXES, None)),
        check_vma=False,
    )
```

```python
import jax
import jax.numpy as jnp
import numpy as np
from jax import lax
from jax.experimental import pallas as pl
from jax.experimental.pallas import tpu as pltpu
from jax.sharding import PartitionSpec as P

NODES = 8
FIELDS = 5
SPAN = 8
DEVICES = 128
POINTS = 16384
CAP = 192
HALF = 64
WIDTH = FIELDS * NODES**3
SLOTS = DEVICES * CAP
GROUP = 64
GROUPS = 16
TILE = 256
ROWS = SLOTS // 256
MOST = SLOTS // TILE + GROUPS
AXES = ("owner", "sub")
F32 = jnp.float32
BF16 = jnp.bfloat16
I32 = jnp.int32


def gll_nodes(count):
    order = count - 1
    points = np.cos(np.pi * np.arange(count) / order)
    for sweep in range(100):
        oldest = np.ones(count)
        recent = points * 1.0
        for degree in range(2, order + 1):
            newest = ((2 * degree - 1) * points * recent - (degree - 1) * oldest) / degree
            oldest = recent
            recent = newest
        points = points - (points * recent - oldest) / (count * recent)
    return points[::-1]


def iota(shape, dim):
    return lax.broadcasted_iota(I32, shape, dim)


def lane_dot(a, b):
    return lax.dot_general(a, b, (((1,), (1,)), ((), ())), preferred_element_type=F32)


def dot(a, b):
    return jnp.dot(a, b, preferred_element_type=F32)


def parts(x):
    high = x.astype(BF16).astype(F32)
    return high, x - high


def earlier(rows, cols):
    return jnp.where(iota((rows, cols), 0) < iota((rows, cols), 1), 1.0, 0.0).astype(BF16)


def packed(value):
    return jnp.broadcast_to(value.astype(F32), (16, value.shape[1])).astype(BF16)


def onehot(first, rows, value):
    value = packed(value)
    base = iota(value.shape, 0)
    one, zero = jnp.asarray(1.0, BF16), jnp.asarray(0.0, BF16)
    out = []
    for r in range(rows // 16):
        out.append(jnp.where((base + (first + 16 * r)).astype(F32).astype(BF16) == value, one, zero))
    return jnp.concatenate(out, axis=0)


def spread(ones, value):
    value = packed(value)
    return jnp.concatenate(
        [ones[16 * r : 16 * r + 16] * value for r in range(ones.shape[0] // 16)], axis=0
    )


def both(ones, high, low):
    return jnp.concatenate([spread(ones, high), spread(ones, low)], axis=1)


def ranks(mask, before, base):
    ones = jnp.where(mask, 1.0, 0.0)
    narrow = ones.astype(BF16)
    counts = []
    rows, blocks = mask.shape[0], mask.shape[1] // 256
    stacked = [narrow[:, 256 * j : 256 * j + 256] for j in range(blocks)]
    stacked = dot(jnp.concatenate(stacked, axis=0), before)
    for j in range(blocks):
        inside = stacked[rows * j : rows * j + rows]
        counts.append(inside + base)
        base = base + inside[:, 255:256] + ones[:, 256 * j + 255 : 256 * j + 256]
    count = jnp.concatenate(counts, axis=1)
    return jnp.sum(jnp.where(mask, count, 0.0), axis=0, keepdims=True), base


def small_ranks(ones, before, base):
    rows, blocks = ones.shape[0], ones.shape[1] // 256
    parts_of = [ones[:, 256 * j : 256 * j + 256] for j in range(blocks)]
    stacked = dot(jnp.concatenate(parts_of, axis=0), before)
    out = []
    for j in range(blocks):
        inside = stacked[rows * j : rows * j + rows]
        count = inside.astype(BF16) + jnp.broadcast_to(base, (rows, 256)).astype(BF16)
        picked = parts_of[j] * count
        total = picked[0:16]
        for r in range(1, rows // 16):
            total = total + picked[16 * r : 16 * r + 16]
        out.append(jnp.sum(total.astype(F32), axis=0, keepdims=True))
        base = base + inside[:, 255:256] + parts_of[j][:, 255:256].astype(F32)
    return jnp.concatenate(out, axis=1), base


def flat_slot(block, place):
    odd = (block & 1) == 1
    late = place >= 128
    return block * CAP + jnp.where(odd, jnp.where(late, place - 128, place + 64), place)


def to_grid(x):
    return ((x + 1.0) * 32767.5 + 0.5).astype(I32).astype(F32)


def from_grid(x):
    return x * (1.0 / 32767.5) - 1.0


def low_half(word):
    return (word << 16) >> 16


def high_half(word):
    return word >> 16


def left_halves(a, b):
    return jnp.where(iota(a.shape, 1) < HALF, a, pltpu.roll(b, HALF, 1))


def right_halves(a, b):
    return jnp.where(iota(a.shape, 1) < HALF, pltpu.roll(a, HALF, 1), b)


A_LANES = 4096


def bucket_kernel(
    dest_hbm, local_hbm, coords_hbm, out_ref, slot_ref, dest_ref, local_ref, coords_ref, acc_ref, flat_ref, sems
):
    early, late = pl.ds(0, A_LANES), pl.ds(A_LANES, POINTS - A_LANES)
    copies = [
        pltpu.make_async_copy(src, dst, sems.at[n])
        for n, (src, dst) in enumerate(
            [
                (local_hbm.at[:, early], local_ref.at[:, early]),
                (local_hbm.at[:, late], local_ref.at[:, late]),
                (dest_hbm, dest_ref),
                (coords_hbm, coords_ref),
            ]
        )
    ]
    for copy in copies:
        copy.start()
    acc_ref[...] = jnp.zeros_like(acc_ref)
    before = earlier(256, 256)
    steps = POINTS // A_LANES

    def at(n):
        return pl.ds(pl.multiple_of(n * A_LANES, A_LANES), A_LANES)

    def place(n, base):
        holder = local_ref[:, at(n)] >> 3
        rank, base = small_ranks(onehot(0, DEVICES, holder), before, base)
        slot_ref[:, at(n)] = flat_slot(holder, rank.astype(I32))
        return base

    def scatter(n):
        slot = slot_ref[:, at(n)]
        where_row = onehot(0, ROWS, slot >> 8)
        where_col = onehot(0, 256, slot & 255)
        local = local_ref[:, at(n)]
        rows = []
        for k in range(3):
            clear = (1 - ((local >> k) & 1)) * 65536
            grid = to_grid(coords_ref[k : k + 1, at(n)]) - clear.astype(F32)
            rows += [spread(where_row, part) for part in parts(grid)]
        rows.append(spread(where_row, dest_ref[:, at(n)] + 1))
        return lane_dot(jnp.concatenate(rows, axis=0), where_col)

    copies[0].wait()
    base = place(0, jnp.zeros((DEVICES, 1), F32))
    for copy in copies[1:]:
        copy.wait()

    def step(n, base):
        got = scatter(n)
        base = place(n + 1, base)
        acc_ref[...] += got
        return base

    lax.fori_loop(0, steps - 1, step, base)
    acc_ref[...] += scatter(steps - 1)
    fields = [acc_ref[k * ROWS : k * ROWS + ROWS, :].astype(I32) for k in range(7)]
    fields = [fields[0] + fields[1], fields[2] + fields[3], fields[4] + fields[5], fields[6]]
    number = fields[3] * 8
    for k in range(3):
        signed = fields[k] + 65536
        number = number + ((signed >> 16) << k)
        fields[k] = signed & 0xFFFF
    fields[3] = jnp.where(fields[3] > 0, number, 0)
    middle = []
    for k in range(2):
        low, high = fields[2 * k], fields[2 * k + 1]
        block = low + (high << 16)
        flat_ref[pl.ds(0, ROWS, 2), :] = block[:, 0:128]
        flat_ref[pl.ds(1, ROWS, 2), :] = block[:, 128:256]
        out_ref[:, k, :] = flat_ref[pl.ds(0, 64, 3), :]
        out_ref[:, 4 + k, :] = flat_ref[pl.ds(2, 64, 3), :]
        middle.append(flat_ref[pl.ds(1, 64, 3), :])
    out_ref[:, 2, :] = left_halves(*middle)
    out_ref[:, 6, :] = right_halves(*middle)
    out_ref[:, 3, :] = jnp.zeros((64, 128), I32)
    out_ref[:, 7, :] = jnp.zeros((64, 128), I32)


def bucket(dest, local, coords):
    return pl.pallas_call(
        bucket_kernel,
        out_shape=(
            jax.ShapeDtypeStruct((DEVICES // 2, 8, 128), I32),
            jax.ShapeDtypeStruct((1, POINTS), I32),
        ),
        in_specs=[pl.BlockSpec(memory_space=pl.ANY)] * 3,
        out_specs=(pl.BlockSpec(memory_space=pltpu.VMEM),) * 2,
        scratch_shapes=[
            pltpu.VMEM((1, POINTS), I32),
            pltpu.VMEM((1, POINTS), I32),
            pltpu.VMEM((3, POINTS), F32),
            pltpu.VMEM((7 * ROWS, 256), F32),
            pltpu.VMEM((2 * ROWS, 128), I32),
            pltpu.SemaphoreType.DMA((4,)),
        ],
        compiler_params=pltpu.CompilerParams(vmem_limit_bytes=56 * 1024 * 1024),
        name="bucket",
    )(dest, local, coords)


SOURCES = 32
C_LANES = SOURCES * CAP
STEPS = DEVICES // SOURCES
USUAL = 96
LEVELS = 32600.0
PAIR = 8
MANY = 16


def basis_rows(x, nodes, scale):
    row = iota((8, x.shape[1]), 0)
    out = None
    for n in range(8):
        term = jnp.where(row == n, scale, x - float(nodes[n]))
        out = term if out is None else out * term
    return out


def evaluate_kernel(
    recv_ref, span_ref, file_hbm, out_ref, file_ref, data_ref, sorted_ref, val_ref, acc_ref, flat_ref, first_ref, group_ref, sem
):
    load = pltpu.make_async_copy(file_hbm, file_ref, sem)
    load.start()
    nodes = gll_nodes(NODES)
    before = earlier(256, 256)
    permutation = jnp.where(iota((128, 128), 0) == span_ref[...], 1.0, 0.0).astype(BF16)
    inverse = lane_dot(iota((16, 128), 1).astype(F32).astype(BF16), permutation).astype(BF16)

    def count(n, base):
        blocks = [recv_ref[n * (SOURCES // 2) + s] for s in range(SOURCES // 2)]
        turned = [pltpu.roll(block, HALF, 1) for block in blocks]
        whole = jnp.concatenate(blocks, axis=1)
        swapped = jnp.concatenate(turned, axis=1)
        early = (iota((1, SOURCES * 64), 1) & 127) < HALF
        words = [
            jnp.concatenate(
                [whole[0:1], whole[4:5], jnp.where(early, whole[2:3], swapped[6:7])], axis=1
            ),
            jnp.concatenate(
                [whole[1:2], whole[5:6], jnp.where(early, swapped[2:3], whole[6:7])], axis=1
            ),
        ]
        number = high_half(words[1])
        span = dot(inverse, onehot(0, 128, (number >> 3) - 1))[0:1].astype(I32)
        group = jnp.where(number > 0, span >> 3, GROUPS)
        element = (span & 7) * 8 + (number & 7)
        rank, base = ranks(iota((GROUPS, C_LANES), 0) == group, before, base)
        lanes = pl.ds(pl.multiple_of(n * C_LANES, C_LANES), C_LANES)
        data_ref[0:1, lanes] = (words[0] & 0xFFFF).astype(F32)
        data_ref[1:2, lanes] = (high_half(words[0]) & 0xFFFF).astype(F32)
        data_ref[2:3, lanes] = (words[1] & 0xFFFF).astype(F32)
        data_ref[3:4, lanes] = element.astype(F32)
        data_ref[4:5, lanes] = group.astype(F32)
        data_ref[5:6, lanes] = rank
        return base

    total = lax.fori_loop(0, STEPS, count, jnp.zeros((GROUPS, 1), F32))
    tiles = ((total.astype(I32) + (TILE - 1)) >> 8).astype(F32)
    lower = jnp.where(iota((GROUPS, GROUPS), 1) < iota((GROUPS, GROUPS), 0), 1.0, 0.0)
    start = dot(lower.astype(BF16), jnp.broadcast_to(tiles, (GROUPS, 128)).astype(BF16))[:, 0:1]
    for g in range(GROUPS):
        first_ref[g] = jnp.sum(start[g : g + 1]).astype(I32)
    first_ref[GROUPS] = jnp.sum(tiles).astype(I32)
    used = first_ref[GROUPS]

    def name_group(g, carry):
        def name_tile(t, inner):
            group_ref[t] = g
            return inner

        return lax.fori_loop(first_ref[g], first_ref[g + 1], name_tile, carry)

    lax.fori_loop(0, GROUPS, name_group, 0)
    for n in range(PAIR - 1):
        group_ref[used + n] = 0

    sorted_ref[...] = jnp.zeros_like(sorted_ref)

    def sort(n, first, rows):
        lanes = pl.ds(pl.multiple_of(n * C_LANES, C_LANES), C_LANES)
        group = data_ref[4:5, lanes].astype(I32)
        here = iota((GROUPS, C_LANES), 0) == group
        base = jnp.sum(jnp.where(here, start, 0.0), axis=0, keepdims=True)
        slot = base.astype(I32) * TILE + data_ref[5:6, lanes].astype(I32)
        where_row = onehot(first, rows, jnp.where(group < GROUPS, slot >> 8, -1))
        where_col = onehot(0, TILE, slot & 255)
        at = iota((1, C_LANES), 1)
        pair = n * (SOURCES // 2) + ((at >> 7) & (SOURCES // 2 - 1))
        third = at >= SOURCES * 128
        odd = jnp.where(third, (at >> 6) & 1, jnp.where(at >= SOURCES * 64, 1, 0))
        back = flat_slot(2 * pair + odd, jnp.where(third, 128 + (at & 63), at & 127))
        lhs = [both(where_row, *parts(data_ref[k : k + 1, lanes])) for k in range(3)]
        lhs.append(both(where_row, ((back >> 8) + 1) * 64, data_ref[3:4, lanes]))
        wide = jnp.concatenate([where_col, where_col], axis=1)
        got = lane_dot(jnp.concatenate(lhs, axis=0), wide)
        last = lane_dot(spread(where_row, back & 255), where_col)
        for k in range(4):
            sorted_ref[k, first : first + rows, :] += got[k * rows : k * rows + rows]
        sorted_ref[4, first : first + rows, :] += last

    def usual(n, carry):
        sort(n, 0, USUAL)
        return carry

    lax.fori_loop(0, STEPS, usual, 0)

    @pl.when(used > USUAL)
    def _():
        def more(n, carry):
            sort(n, USUAL, MOST - USUAL)
            return carry

        lax.fori_loop(0, STEPS, more, 0)

    val_ref[...] = jnp.zeros_like(val_ref)
    load.wait()
    row8 = iota((8, TILE), 0)
    scales = jnp.zeros((8, TILE), F32)
    for i in range(8):
        value = 1.0
        for n in range(8):
            if n != i:
                value = value / (nodes[i] - nodes[n])
        scales = jnp.where(row8 == i, float(value), scales)

    def one_tile(t):
        rows = pl.ds(pl.multiple_of(group_ref[t] * GROUP, GROUP), GROUP)
        table = jnp.concatenate(
            [file_ref[rows, f * 512 : f * 512 + 512] for f in range(FIELDS)], axis=0
        )
        table = jnp.concatenate([table, table], axis=1)
        b0, b1, b2 = [basis_rows(from_grid(sorted_ref[k, pl.ds(t, 1), :]), nodes, scales) for k in range(3)]
        element = sorted_ref[3, pl.ds(t, 1), :].astype(I32) & 63
        planes = jnp.concatenate([b1[j : j + 1] * b2 for j in range(8)], axis=0)
        tops, lows = [], []
        for i in range(8):
            tensor = b0[i : i + 1] * planes
            top = tensor.astype(BF16)
            tops.append(top)
            lows.append((tensor - top.astype(F32)).astype(BF16))
        result = dot(table, jnp.concatenate(tops + lows, axis=0))
        mask = iota((GROUP, TILE), 0) == element
        return [
            jnp.sum(
                jnp.where(mask, result[f * GROUP : f * GROUP + GROUP], 0.0), axis=0, keepdims=True
            )
            for f in range(FIELDS)
        ]

    def on_tiles(n, carry):
        values = [one_tile(n * PAIR + q) for q in range(PAIR)]
        for q in range(PAIR):
            for f in range(FIELDS):
                val_ref[f, pl.ds(n * PAIR + q, 1), :] = values[q][f]
        return carry

    lax.fori_loop(0, (used + PAIR - 1) // PAIR, on_tiles, 0)

    acc_ref[...] = jnp.zeros_like(acc_ref)

    def back(n, carry):
        def row(ref, k):
            lines = [ref[k, pl.ds(n * MANY + q, 1), :] for q in range(MANY)]
            return jnp.concatenate(lines, axis=1)

        where_row = onehot(0, ROWS, (row(sorted_ref, 3).astype(I32) >> 6) - 1)
        where_col = onehot(0, 256, row(sorted_ref, 4))
        wide = jnp.concatenate([where_col, where_col], axis=1)
        lhs = [both(where_row, *parts(row(val_ref, f))) for f in range(FIELDS)]
        acc_ref[...] += lane_dot(jnp.concatenate(lhs, axis=0), wide)
        return carry

    lax.fori_loop(0, (used + MANY - 1) // MANY, back, 0)
    evens, odds, middle = [], [], []
    for f in range(FIELDS):
        block = acc_ref[f * ROWS : f * ROWS + ROWS, :]
        flat_ref[pl.ds(0, ROWS, 2), :] = block[:, 0:128]
        flat_ref[pl.ds(1, ROWS, 2), :] = block[:, 128:256]
        evens.append(flat_ref[pl.ds(0, 64, 3), :])
        odds.append(flat_ref[pl.ds(2, 64, 3), :])
        middle.append(flat_ref[pl.ds(1, 64, 3), :])
    low = iota((64, 128), 1) < HALF

    def exponent(firsts, own):
        most = jnp.zeros((64, 128), F32)
        for first, mid in zip(firsts, middle):
            most = jnp.maximum(most, jnp.abs(first))
            most = jnp.maximum(most, jnp.where(own, jnp.abs(mid), 0.0))
        most = jnp.max(most, axis=1, keepdims=True)
        power = jnp.ceil(jnp.log2(jnp.maximum(most, 1e-30)))
        return jnp.broadcast_to(power, (64, 128))

    def coded(value, factor):
        return jnp.floor(value * factor + 0.5).astype(I32)

    def word(a, b):
        return (a & 0xFFFF) | (b << 16)

    powers = [exponent(evens, low), exponent(odds, jnp.logical_not(low))]
    factors = [LEVELS * jnp.exp2(-power) for power in powers]
    last = [coded(mid, jnp.where(low, factors[0], factors[1])) for mid in middle]
    for odd, firsts in enumerate((evens, odds)):
        halves = right_halves if odd else left_halves
        first = [coded(value, factors[odd]) for value in firsts]
        power = powers[odd].astype(I32)
        out_ref[:, 4 * odd, :] = word(first[0], first[1])
        out_ref[:, 4 * odd + 1, :] = word(first[2], first[3])
        out_ref[:, 4 * odd + 2, :] = word(first[4], halves(last[0], last[1]))
        tail = pltpu.roll(last[3], HALF, 1) if odd else last[3]
        out_ref[:, 4 * odd + 3, :] = word(halves(last[2], last[4]), jnp.where(low, tail, power))


def evaluate(recv, span, file_fields):
    return pl.pallas_call(
        evaluate_kernel,
        out_shape=jax.ShapeDtypeStruct((DEVICES // 2, 8, 128), I32),
        in_specs=[
            pl.BlockSpec(memory_space=pltpu.VMEM),
            pl.BlockSpec(memory_space=pltpu.VMEM),
            pl.BlockSpec(memory_space=pl.ANY),
        ],
        out_specs=pl.BlockSpec(memory_space=pltpu.VMEM),
        scratch_shapes=[
            pltpu.VMEM((DEVICES * SPAN, WIDTH), BF16),
            pltpu.VMEM((8, SLOTS), F32),
            pltpu.VMEM((5, MOST, TILE), F32),
            pltpu.VMEM((FIELDS, MOST, TILE), F32),
            pltpu.VMEM((FIELDS * ROWS, 256), F32),
            pltpu.VMEM((2 * ROWS, 128), F32),
            pltpu.SMEM((GROUPS + 1,), I32),
            pltpu.SMEM((MOST + PAIR,), I32),
            pltpu.SemaphoreType.DMA(()),
        ],
        compiler_params=pltpu.CompilerParams(vmem_limit_bytes=50 * 1024 * 1024),
        cost_estimate=pl.CostEstimate(
            flops=60_000_000_000, bytes_accessed=6_000_000, transcendentals=0
        ),
        name="evaluate",
    )(recv, span, file_fields)


E_LANES = 2048
PIECES = 4


def collect_kernel(
    back_ref, slot_ref, moved_hbm, out_ref, owned_hbm, table_ref, flat_ref, held_ref, sems
):
    rows = DEVICES * SPAN // PIECES
    pieces = [pl.ds(n * rows, rows) for n in range(PIECES)]
    loads = [
        pltpu.make_async_copy(moved_hbm.at[p], held_ref.at[p], sems.at[n])
        for n, p in enumerate(pieces)
    ]
    stores = [
        pltpu.make_async_copy(held_ref.at[p], owned_hbm.at[p], sems.at[PIECES + n])
        for n, p in enumerate(pieces)
    ]
    for copy in loads:
        copy.start()
    firsts, lasts = [], []
    for odd in range(2):
        words = [back_ref[:, 4 * odd + r, :] for r in range(4)]
        tail = high_half(words[3])
        factor = jnp.exp2(right_halves(tail, tail).astype(F32)) * (1.0 / LEVELS)
        firsts.append(
            [
                half(words[r]).astype(F32) * factor
                for r, half in (
                    (0, low_half), (0, high_half), (1, low_half), (1, high_half), (2, low_half)
                )
            ]
        )
        lasts.append(
            [
                value.astype(F32) * factor
                for value in (high_half(words[2]), low_half(words[3]), tail)
            ]
        )
    for f in range(FIELDS):
        flat_ref[pl.ds(0, 64, 3), :] = firsts[0][f]
        flat_ref[pl.ds(2, 64, 3), :] = firsts[1][f]
        k, halves = ((0, left_halves), (0, right_halves), (1, left_halves), (2, left_halves), (1, right_halves))[f]
        flat_ref[pl.ds(1, 64, 3), :] = halves(lasts[0][k], lasts[1][k])
        for half in range(2):
            high, rest = parts(flat_ref[pl.ds(half, ROWS, 2), :])
            here = slice(f * ROWS, f * ROWS + ROWS)
            table_ref[here, 128 * half : 128 * half + 128] = high.astype(BF16)
            table_ref[here, 256 + 128 * half : 384 + 128 * half] = rest.astype(BF16)

    def step(n, carry):
        lanes = pl.ds(pl.multiple_of(n * E_LANES, E_LANES), E_LANES)
        slot = slot_ref[:, lanes]
        mask = iota((ROWS, E_LANES), 0) == (slot >> 8)
        where_col = onehot(0, 256, slot & 255)
        got = dot(table_ref[...], jnp.concatenate([where_col, where_col], axis=0))
        for f in range(FIELDS):
            out_ref[f : f + 1, lanes] = jnp.sum(
                jnp.where(mask, got[f * ROWS : f * ROWS + ROWS], 0.0), axis=0, keepdims=True
            )
        return carry

    steps = POINTS // E_LANES
    lax.fori_loop(0, steps // 2, step, 0, unroll=True)
    for load, store in zip(loads, stores):
        load.wait()
        store.start()
    lax.fori_loop(steps // 2, steps, step, 0, unroll=True)
    for store in stores:
        store.wait()


def collect(back, slot, moved):
    return pl.pallas_call(
        collect_kernel,
        out_shape=(
            jax.ShapeDtypeStruct((FIELDS, POINTS), F32),
            jax.ShapeDtypeStruct(moved.shape, moved.dtype),
        ),
        in_specs=[
            pl.BlockSpec(memory_space=pltpu.VMEM),
            pl.BlockSpec(memory_space=pltpu.VMEM),
            pl.BlockSpec(memory_space=pl.ANY),
        ],
        out_specs=(pl.BlockSpec(memory_space=pltpu.VMEM), pl.BlockSpec(memory_space=pl.ANY)),
        scratch_shapes=[
            pltpu.VMEM((FIELDS * ROWS, 512), BF16),
            pltpu.VMEM((2 * ROWS, 128), F32),
            pltpu.VMEM((DEVICES * SPAN, WIDTH), BF16),
            pltpu.SemaphoreType.DMA((2 * PIECES,)),
        ],
        compiler_params=pltpu.CompilerParams(vmem_limit_bytes=56 * 1024 * 1024),
        name="collect",
    )(back, slot, moved)


def exchange(x):
    return lax.all_to_all(x, AXES, split_axis=0, concat_axis=0, tiled=True)


def shards(file_fields, span_map, point_dest, point_local, point_coords):
    columns = jnp.arange(DEVICES, dtype=I32)
    inverse = jnp.zeros((DEVICES,), I32).at[span_map[0]].set(columns)
    pieces = file_fields.reshape(DEVICES, SPAN, WIDTH)[inverse]
    sent, slot = bucket(
        point_dest.reshape(1, POINTS), point_local.reshape(1, POINTS), point_coords
    )
    recv = exchange(sent.reshape(DEVICES, 4, 128)).reshape(DEVICES // 2, 8, 128)
    pieces, recv = lax.optimization_barrier((pieces, recv))
    moved = exchange(pieces).reshape(DEVICES * SPAN, WIDTH)
    values = evaluate(recv, span_map, file_fields)
    values, moved = lax.optimization_barrier((values, moved))
    back = exchange(values.reshape(DEVICES, 4, 128)).reshape(DEVICES // 2, 8, 128)
    return collect(back, slot, moved)


def solution(mesh):
    return jax.shard_map(
        shards,
        mesh=mesh,
        in_specs=(
            P(AXES, None),
            P(AXES, None),
            P(AXES, None),
            P(AXES),
            P(None, AXES),
        ),
        out_specs=(P(None, AXES), P(AXES, None)),
        check_vma=False,
    )
```
